512 devices in a mesh: cuts: 16 (over z_lo, y), energy: 32 (over x, z_hi, core).
Axes of the slice: x: 4, y: 4, z: 16 (z_hi: 4, z_lo: 4; z = z_hi * 4 + z_lo), core: 2. Of those that a mesh axis runs over, the one named last changes fastest.
Arguments:
- inverse: bfloat16 [2, 64, 16, 512, 512], P(None, 'energy', 'cuts'), may hold values from -3 to 3
- coupling: bfloat16 [2, 16, 512, 512], P(None, 'cuts'), may hold values from -0.15625 to 0.15625
- pattern: int32 [16, 4, 4], P('cuts'), may hold values 0 or 1
- source: bfloat16 [2, 64, 16, 96, 512], P(None, 'energy', 'cuts'), may hold values from -6 to 6
- previous: bfloat16 [2, 64, 16, 96, 512], P(None, 'energy', 'cuts'), may hold values from -6 to 6
- offsets: int32 [4], replicated, may hold values from 1 to 2, as said below
- strength: float32 [4], replicated, may hold values from 0.2 to 0.5
Outputs:
- updated: bfloat16 [2, 64, 16, 96, 512], P(None, 'energy', 'cuts')
The draws below stay inside these ranges and needn't reach their ends.
Inputs may be any that keep to these rules, and one draw needn't show every extreme that they name: One of the offsets equals 2.
All inputs are finite; a program needn't handle non-finite values. No bound on the sum of `pattern` on one device may be relied on, other than what follows from the above.
Results may differ from the reference program's by a relative error of at most 0.035.
Values may be sent and summed in bfloat16 or wider, within the bound.
A program may use at most 64 MiB of HBM per device.

```python
import math
import jax
import jax.numpy as jnp
from jax import lax

NO = 512
NB = 4
NR = 96
E_DEV = 2
MODES = 4
NE = 64
NS = 16


def draw_inverse(key, part):
    first, second, third = jax.random.split(key, 3)
    diagonal_values = jax.random.uniform(first, (NE, NS, NO), jnp.float32, 0.5, 1.5)
    spread = jax.random.normal(second, (2, NE, NS, NO, NO), jnp.float32) * (0.3 / NO ** 0.5)
    imag_diagonal = jax.random.uniform(third, (NE, NS, NO), jnp.float32, -0.4, 0.4)
    identity = jnp.eye(NO, dtype=jnp.float32)
    real_block = spread[0] + diagonal_values[..., None] * identity
    imag_block = spread[1] + imag_diagonal[..., None] * identity
    return jnp.stack([real_block, imag_block]).astype(jnp.bfloat16)


def draw_offsets(key, part):
    key = jax.random.fold_in(key, 7)
    first, second = jax.random.split(key)
    drawn = jax.random.randint(first, (MODES,), 1, E_DEV + 1)
    chosen = jax.random.randint(second, (), 0, MODES)
    return jnp.where(jnp.arange(MODES) == chosen, E_DEV, drawn).astype(jnp.int32)


def touch_ends(values, rng, least, top_value):
    longest = values.shape.index(max(values.shape))
    spots = []
    for shift in (0, 1):
        where = [jax.random.randint(jax.random.fold_in(rng, axis), (), 0, length) for axis, length in enumerate(values.shape)]
        where[longest] = (where[longest] + shift) % values.shape[longest]
        spots.append(tuple(where))
    return values.at[spots[0]].set(least).at[spots[1]].set(top_value)


def steps_of(rng, dims, cuts, low, high):
    gain, own = 1.0, jax.random.fold_in(rng, 6)
    for dim, blocks in cuts:
        steps = jnp.exp(jax.random.uniform(jax.random.fold_in(own, dim), (blocks,), jnp.float32, low / len(cuts), high / len(cuts)))
        gain = gain * jnp.repeat(steps, dims[dim] // blocks).reshape([-1 if axis == dim else 1 for axis in range(len(dims))])
    return gain


def noise(rng, shape, width, bound, pieces=(), kind=jnp.bfloat16):
    gain = steps_of(rng, shape, pieces, -0.22, 0.18) if pieces else 1.0
    values = jax.random.normal(rng, shape, jnp.float32) * width * gain
    return jnp.minimum(jnp.maximum(values, -bound), bound).astype(kind)


def setup_inputs(seed: int = 0) -> dict:
    streams_of = jax.random.split(jax.random.key(seed), 8)
    inverse = draw_inverse(jax.random.fold_in(streams_of[7], 71), 0)
    coupling = noise(streams_of[1], (2, NS, NO, NO), (5 * NO // 2) ** -0.5, 0.15625, ((1, 16),))
    pattern = touch_ends((jax.random.randint(streams_of[2], (NS, NB, NB), 0, 4) < 3).astype(jnp.int32), jax.random.fold_in(streams_of[2], 1), 0, 1)
    source = noise(streams_of[3], (2, NE, NS, NR, NO), 1.0, 6.0, ((1, 32), (2, 16)))
    previous = noise(streams_of[4], (2, NE, NS, NR, NO), 1.0, 6.0, ((1, 32), (2, 16)))
    offsets = draw_offsets(jax.random.fold_in(streams_of[7], 71), 0)
    strength = jnp.clip(jnp.exp(jax.random.uniform(streams_of[6], (MODES,), jnp.float32, math.log(0.2), math.log(0.5))), 0.2, 0.5)
    return {"inverse": inverse, "coupling": coupling, "pattern": pattern, "source": source, "previous": previous, "offsets": offsets, "strength": strength}


def expand_pattern(coupling, pattern):
    blocks = pattern.shape[-1]
    block_width = coupling.shape[-1] // blocks
    shaped = coupling.reshape(coupling.shape[:-2] + (blocks, block_width, blocks, block_width))
    block_mask = pattern.astype(coupling.dtype)[..., :, None, :, None]
    return (shaped * block_mask).reshape(coupling.shape)


def times_inverse(matrix, vector):
    matrix32 = matrix.astype(jnp.float32)
    vector32 = vector.astype(jnp.float32)
    with_real = jnp.einsum('cero,epo->cerp', vector32, matrix32[0])
    with_imag = jnp.einsum('cero,epo->cerp', vector32, matrix32[1])
    return jnp.stack([with_real[0] - with_imag[1], with_real[1] + with_imag[0]])


def couple(matrix, vector):
    matrix32 = matrix.astype(jnp.float32)
    vector32 = vector.astype(jnp.float32)
    with_real = jnp.einsum('cero,po->cerp', vector32, matrix32[0])
    with_imag = jnp.einsum('cero,po->cerp', vector32, matrix32[1])
    return jnp.stack([with_real[0] - with_imag[1], with_real[1] + with_imag[0]])


def couple_adjoint(matrix, vector):
    matrix32 = matrix.astype(jnp.float32)
    vector32 = vector.astype(jnp.float32)
    with_real = jnp.einsum('cero,op->cerp', vector32, matrix32[0])
    with_imag = jnp.einsum('cero,op->cerp', vector32, matrix32[1])
    return jnp.stack([with_real[0] + with_imag[1], with_real[1] - with_imag[0]])


def photon_drive(source, previous, offsets, strength):
    margin = E_DEV
    padded = jnp.pad(previous.astype(jnp.float32), ((0, 0), (margin, margin), (0, 0), (0, 0), (0, 0)))
    summed = source.astype(jnp.float32)
    for channel in range(MODES):
        offset_now = offsets[channel].astype(jnp.int32)
        above_energy = lax.dynamic_slice_in_dim(padded, margin + offset_now, NE, 1)
        below_energy = lax.dynamic_slice_in_dim(padded, margin - offset_now, NE, 1)
        summed = summed + strength[channel] * (above_energy + below_energy)
    return summed.astype(jnp.bfloat16)


def reference(inverse, coupling, pattern, source, previous, offsets, strength):
    drive_term = photon_drive(source, previous, offsets, strength)
    masked = expand_pattern(coupling, pattern[None])
    carried_state = jnp.zeros((2, NE, NR, NO), jnp.bfloat16)
    forward = []
    for cut_index in range(NS):
        step_term = drive_term[:, :, cut_index].astype(jnp.float32) - couple(masked[:, cut_index], carried_state)
        step_term = step_term.astype(jnp.bfloat16)
        carried_state = times_inverse(inverse[:, :, cut_index], step_term).astype(jnp.bfloat16)
        forward.append(carried_state)
    carried = jnp.zeros((2, NE, NR, NO), jnp.bfloat16)
    result = [None] * NS
    for cut_index in reversed(range(NS)):
        newest = forward[cut_index].astype(jnp.float32) - times_inverse(inverse[:, :, cut_index], carried)
        newest = newest.astype(jnp.bfloat16)
        result[cut_index] = newest
        carried = couple_adjoint(masked[:, cut_index], newest).astype(jnp.bfloat16)
    return jnp.stack(result, axis=2)
```

```python
import functools

import jax
import jax.numpy as jnp
from jax import lax
from jax.experimental import pallas as pl
from jax.experimental.pallas import tpu as pltpu
from jax.sharding import PartitionSpec as P

MESH = pl.DeviceIdType.MESH
F32 = jnp.float32
BF16 = jnp.bfloat16
ROWS = 16
SPAN = 4


def combined(product):
    h, w = product.shape[0] // 2, product.shape[1] // 2
    real = product[:h, :w] - product[h:, w:]
    imag = product[:h, w:] + product[h:, :w]
    return real, imag


def sweep_kernel(
    cuts, energies, inv_ref, cpl_ref, pat_ref, src_ref, prev_ref, off_ref, str_ref, out_ref,
    inv_v, it_v, cpl_v, cm_v, cmt_v, cm1_v, wf_v, we_v, src_v, prev_v, hl_v, hr_v,
    x_v, fin_v, u_v, bin_v,
    load_sem, hs_l, hs_r, hr_l, hr_r, cm_s, cm_r, wf_s, wf_r, we_s, we_r, a_s, a_r,
    f_s, f_r, b_s, b_r, o_s, o_r, turn_sem,
):
    blocks = pat_ref.shape[-1]
    no = inv_v.shape[-1]
    half = no // 2
    nb = no // blocks
    row_blocks = src_v.shape[2] // ROWS
    chunks = 4 * row_blocks
    pos = lax.axis_index("cuts")
    e = lax.axis_index("energy")
    core = lax.rem(e, 2)
    last = cuts - 1

    def rows(rb):
        return pl.ds(pl.multiple_of(rb * ROWS, ROWS), ROWS)

    def remote(src, dst, send, recv, device):
        return pltpu.make_async_remote_copy(
            src_ref=src, dst_ref=dst, send_sem=send, recv_sem=recv,
            device_id=device, device_id_type=MESH,
        )

    load_cpl = pltpu.make_async_copy(cpl_ref.at[:, 0], cpl_v, load_sem.at[0])
    load_inv = [
        pltpu.make_async_copy(inv_ref.at[:, l, 0], inv_v.at[l], load_sem.at[1 + l]) for l in range(2)
    ]
    load_src = pltpu.make_async_copy(src_ref.at[:, :, 0], src_v, load_sem.at[3])
    load_prev = pltpu.make_async_copy(prev_ref.at[:, :, 0], prev_v, load_sem.at[4])
    load_cpl.start()
    for copy in load_inv:
        copy.start()
    load_src.start()
    load_prev.start()

    barrier = pltpu.get_barrier_semaphore()
    partners = (
        (pos > 0, {"cuts": pos - 1}),
        (pos < last, {"cuts": pos + 1}),
        (e > 0, {"energy": e - 1}),
        (e < energies - 1, {"energy": e + 1}),
        (pos >= SPAN, {"cuts": pos - SPAN}),
        (pos < cuts - SPAN, {"cuts": pos + SPAN}),
    )
    for there, device in partners:
        @pl.when(there)
        def _():
            pl.semaphore_signal(barrier, inc=1, device_id=device, device_id_type=MESH)
    pl.semaphore_wait(barrier, sum(jnp.where(there, 1, 0) for there, _ in partners))

    def halo_right(rb):
        return remote(prev_ref.at[:, :, 0, rows(rb)], hl_v.at[:, :, rows(rb)], hs_r.at[rb], hr_l.at[rb], {"energy": e + 1})

    def halo_left(rb):
        return remote(prev_ref.at[:, :, 0, rows(rb)], hr_v.at[:, :, rows(rb)], hs_l.at[rb], hr_r.at[rb], {"energy": e - 1})

    def start_halo():
        @pl.loop(0, row_blocks)
        def _(rb):
            @pl.when(e < energies - 1)
            def _():
                halo_right(rb).start()

            @pl.when(e > 0)
            def _():
                halo_left(rb).start()

    @pl.when(e == 0)
    def _():
        hl_v[...] = jnp.zeros(hl_v.shape, BF16)

    @pl.when(e == energies - 1)
    def _():
        hr_v[...] = jnp.zeros(hr_v.shape, BF16)

    @pl.when(pos < SPAN)
    def _():
        start_halo()

    load_cpl.wait()
    for a in range(blocks):
        for b in range(blocks):
            keep = pat_ref[0, a, b].astype(F32)
            t, top = divmod(a * nb, half)
            lanes = slice(b * nb, (b + 1) * nb)
            real = cpl_v[0, a * nb:(a + 1) * nb, lanes].astype(F32)
            imag = cpl_v[1, a * nb:(a + 1) * nb, lanes].astype(F32)
            cm_v[t, top:top + nb, lanes] = (real * (-keep)).astype(BF16)
            cm_v[t, half + top:half + top + nb, lanes] = (imag * keep).astype(BF16)
    send_cm = remote(cm_v, cm1_v, cm_s, cm_r, {"cuts": pos - 1})

    @pl.when(lax.rem(pos, SPAN) != 0)
    def _():
        send_cm.start()

    for l in range(2):
        load_inv[l].wait()
        it_v[l, :, :no] = inv_v[l, 0].T
        it_v[l, :, no:] = inv_v[l, 1].T

    def product_into(left, right_l, target, slot):
        @pl.loop(0, 2)
        def _(t):
            product = jnp.dot(left[t], it_v[right_l], preferred_element_type=F32)
            real, imag = combined(product)
            top = pl.ds(pl.multiple_of(t * half, half), half)
            target[slot, top, :no] = real.astype(BF16)
            target[slot, top, no:] = imag.astype(BF16)

    def to_mate(ref, slot, send, recv):
        return remote(ref.at[slot], ref.at[slot], send, recv, {"energy": e + 1})

    @pl.when(pos > 0)
    def _():
        for t in range(2):
            lanes = slice(t * half, (t + 1) * half)
            real = cm_v[t, :half, :].T
            imag = -(cm_v[t, half:, :].T)
            for s in range(2):
                cmt_v[s, :half, lanes] = real[s * half:(s + 1) * half]
                cmt_v[s, half:, lanes] = imag[s * half:(s + 1) * half]

        @pl.loop(0, 2)
        def _(l):
            product_into(cmt_v, l, wf_v, 2 * core + l)

            @pl.when(core == 0)
            def _():
                to_mate(wf_v, l, wf_s.at[l], wf_r.at[l]).start()

    @pl.when(pos >= SPAN)
    def _():
        pl.semaphore_wait(turn_sem, 1)
        start_halo()

    @pl.when((pos > 0) & (lax.rem(pos, SPAN) == 0))
    def _():
        send_cm.start()

    near = F32(0)
    far = F32(0)
    for mode in range(off_ref.shape[0]):
        near = near + jnp.where(off_ref[mode] == 1, str_ref[mode], F32(0))
        far = far + jnp.where(off_ref[mode] == 2, str_ref[mode], F32(0))
    load_src.wait()
    load_prev.wait()

    def send_forward(n):
        return remote(x_v.at[n], fin_v.at[n], f_s.at[n], f_r.at[n], {"cuts": pos + 1})

    def send_backward(ref, n):
        return remote(ref.at[n], bin_v.at[n], b_s.at[n], b_r.at[n], {"cuts": pos - 1})

    def send_a(rb, l):
        return remote(x_v.at[4 * rb + l], x_v.at[4 * rb + l], a_s.at[2 * rb + l], a_r.at[2 * rb + l], {"energy": e + 1})

    @pl.loop(0, row_blocks)
    def _(rb):
        at = rows(rb)

        @pl.when(e > 0)
        def _():
            halo_right(rb).wait_recv()

        @pl.when(e < energies - 1)
        def _():
            halo_left(rb).wait_recv()

        @pl.when((rb == 1) & (pos < cuts - SPAN))
        def _():
            pl.semaphore_signal(turn_sem, inc=1, device_id={"cuts": pos + SPAN}, device_id_type=MESH)

        own = [prev_v[:, l, at, :].astype(F32) for l in range(2)]
        lo = [hl_v[:, l, at, :].astype(F32) for l in range(2)]
        hi = [hr_v[:, l, at, :].astype(F32) for l in range(2)]
        drives = (
            src_v[:, 0, at, :].astype(F32) + near * (own[1] + lo[1]) + far * (hi[0] + lo[0]),
            src_v[:, 1, at, :].astype(F32) + near * (hi[0] + own[0]) + far * (hi[1] + lo[1]),
        )
        for l in range(2):
            left = drives[l].astype(BF16).reshape(2 * ROWS, no)
            real, imag = combined(jnp.dot(left, it_v[l], preferred_element_type=F32))
            n = 4 * rb + 2 * core + l
            x_v[n, 0] = real.astype(BF16)
            x_v[n, 1] = imag.astype(BF16)

            @pl.when(core == 0)
            def _():
                send_a(rb, l).start()

            @pl.when((core == 1) & (pos == 0))
            def _():
                send_forward(n).start()

        @pl.when((core == 1) & (pos == 0))
        def _():
            for l in range(2):
                send_a(rb, l).wait_recv()
                send_forward(4 * rb + l).start()

    def own_we():
        remote(cm_v, cm1_v, cm_s, cm_r, {"cuts": pos - 1}).wait_recv()

        @pl.loop(0, 2)
        def _(l):
            product_into(cm1_v, l, we_v, 2 * core + l)

            @pl.when(core == 0)
            def _():
                to_mate(we_v, l, we_s.at[l], we_r.at[l]).start()

    def out_mate(ref, n):
        rb, slot = lax.div(n, 4), lax.rem(n, 4)
        return remote(
            ref.at[n], out_ref.at[:, slot, 0, rows(rb)], o_s.at[n], o_r.at[2 * rb + slot], {"energy": e - 1}
        )

    def out_own(ref, n):
        rb, slot = lax.div(n, 4), lax.rem(n, 4)
        return pltpu.make_async_copy(ref.at[n], out_ref.at[:, slot - 2, 0, rows(rb)], o_s.at[n])

    def write_out(ref, n):
        @pl.when(lax.rem(n, 4) < 2)
        def _():
            out_mate(ref, n).start()

        @pl.when(lax.rem(n, 4) >= 2)
        def _():
            out_own(ref, n).start()

    def stepped(given, weights, added, n):
        left = given[n].reshape(2 * ROWS, no)
        real, imag = combined(jnp.dot(left, weights[lax.rem(n, 4)], preferred_element_type=F32))
        return (real + added[n, 0].astype(F32)).astype(BF16), (imag + added[n, 1].astype(F32)).astype(BF16)

    def forward_step(n):
        @pl.when(n < 2)
        def _():
            to_mate(wf_v, n, wf_s.at[n], wf_r.at[n]).wait_recv()

        @pl.when(lax.rem(n, 4) < 2)
        def _():
            send_a(lax.div(n, 4), lax.rem(n, 4)).wait_recv()

        send_forward(n).wait_recv()
        x_v[n, 0], x_v[n, 1] = stepped(fin_v, wf_v, x_v, n)

        @pl.when(pos < last)
        def _():
            send_forward(n).start()

        @pl.when(pos == last)
        def _():
            send_backward(x_v, n).start()
            write_out(x_v, n)

    def backward_step(n):
        @pl.when(n < 2)
        def _():
            to_mate(we_v, n, we_s.at[n], we_r.at[n]).wait_recv()

        send_backward(u_v, n).wait_recv()
        u_v[n, 0], u_v[n, 1] = stepped(bin_v, we_v, x_v, n)

        @pl.when(pos > 0)
        def _():
            send_backward(u_v, n).start()

        write_out(u_v, n)

    lag = jnp.minimum(7 * (last - pos), chunks)

    def tick(n, _):
        @pl.when((n < chunks) & (pos > 0))
        def _():
            forward_step(n)

        @pl.when((n >= lag) & (pos < last))
        def _():
            backward_step(n - lag)

        return 0

    split = jnp.where(lag < chunks, 0, chunks)

    @pl.when(core == 1)
    def _():
        lax.fori_loop(0, split, tick, 0)

    @pl.when(pos < last)
    def _():
        own_we()

    @pl.when(core == 1)
    def _():
        lax.fori_loop(split, chunks + lag, tick, 0)

    @pl.when(core == 0)
    def _():
        @pl.loop(0, row_blocks)
        def _(rb):
            for l in range(2):
                remote(
                    u_v.at[4 * rb + l], out_ref.at[:, l, 0, rows(rb)], o_s.at[4 * rb + l], o_r.at[2 * rb + l],
                    {"energy": e + 1},
                ).wait_recv()
                send_a(rb, l).wait_send()

        for l in range(2):
            @pl.when(pos > 0)
            def _():
                to_mate(wf_v, l, wf_s.at[l], wf_r.at[l]).wait_send()

            @pl.when(pos < last)
            def _():
                to_mate(we_v, l, we_s.at[l], we_r.at[l]).wait_send()

    @pl.when(core == 1)
    def _():
        @pl.loop(0, chunks)
        def _(n):
            @pl.when(pos < last)
            def _():
                send_forward(n).wait_send()

            @pl.when(pos > 0)
            def _():
                send_backward(u_v, n).wait_send()

            @pl.when(lax.rem(n, 4) < 2)
            def _():
                out_mate(u_v, n).wait_send()

            @pl.when(lax.rem(n, 4) >= 2)
            def _():
                out_own(u_v, n).wait()

    @pl.loop(0, row_blocks)
    def _(rb):
        @pl.when(e < energies - 1)
        def _():
            halo_right(rb).wait_send()

        @pl.when(e > 0)
        def _():
            halo_left(rb).wait_send()

    @pl.when(pos > 0)
    def _():
        send_cm.wait_send()


def on_device(cuts, energies, inverse, coupling, pattern, source, previous, offsets, strength):
    no, nr = source.shape[4], source.shape[3]
    row_blocks = nr // ROWS
    chunks = 4 * row_blocks
    dma = pltpu.SemaphoreType.DMA
    panel = pltpu.VMEM((2, 2, nr, no), BF16)
    pieces = pltpu.VMEM((chunks, 2, ROWS, no), BF16)
    stack = pltpu.VMEM((2, no, no), BF16)
    anywhere = pl.BlockSpec(memory_space=pl.ANY)
    scalars = pl.BlockSpec(memory_space=pltpu.SMEM)
    return pl.pallas_call(
        functools.partial(sweep_kernel, cuts, energies),
        name="sweeps",
        out_shape=jax.ShapeDtypeStruct(source.shape, BF16),
        in_specs=[anywhere, anywhere, scalars, anywhere, anywhere, scalars, scalars],
        out_specs=anywhere,
        scratch_shapes=[
            pltpu.VMEM((2, 2, no, no), BF16),
            pltpu.VMEM((2, no, 2 * no), BF16),
            stack, stack, stack, stack,
            pltpu.VMEM((4, no, 2 * no), BF16),
            pltpu.VMEM((4, no, 2 * no), BF16),
            panel, panel, panel, panel,
            pieces, pieces, pieces, pieces,
            dma((5,)),
            dma((row_blocks,)), dma((row_blocks,)), dma((row_blocks,)), dma((row_blocks,)),
            dma, dma,
            dma((2,)), dma((2,)), dma((2,)), dma((2,)),
            dma((2 * row_blocks,)), dma((2 * row_blocks,)),
            dma((chunks,)), dma((chunks,)), dma((chunks,)), dma((chunks,)),
            dma((chunks,)), dma((2 * row_blocks,)),
            pltpu.SemaphoreType.REGULAR,
        ],
        compiler_params=pltpu.CompilerParams(
            collective_id=0, has_side_effects=True, vmem_limit_bytes=48 << 20
        ),
    )(inverse, coupling, pattern, source, previous, offsets, strength)


def solution(mesh):
    return jax.shard_map(
        functools.partial(on_device, mesh.shape["cuts"], mesh.shape["energy"]),
        mesh=mesh,
        in_specs=(
            P(None, "energy", "cuts", None, None),
            P(None, "cuts", None, None),
            P("cuts", None, None),
            P(None, "energy", "cuts", None, None),
            P(None, "energy", "cuts", None, None),
            P(),
            P(),
        ),
        out_specs=P(None, "energy", "cuts", None, None),
        check_vma=False,
    )
```

```python
import functools

import jax
import jax.numpy as jnp
from jax import lax
from jax.experimental import pallas as pl
from jax.experimental.pallas import tpu as pltpu
from jax.sharding import PartitionSpec as P

MESH = pl.DeviceIdType.MESH
F32 = jnp.float32
BF16 = jnp.bfloat16
SPAN = 4
PARTS = 2


def combined(product):
    h, w = product.shape[0] // 2, product.shape[1] // 2
    real = product[:h, :w] - product[h:, w:]
    imag = product[:h, w:] + product[h:, :w]
    return real, imag


def sweep_kernel(
    cuts, energies, inv_ref, cpl_ref, pat_ref, src_ref, prev_ref, off_ref, str_ref, out_ref,
    inv_v, it_v, cpl_v, cm_v, cmt_v, cm1_v, wfo_v, weo_v, wf_v, we_v, src_v, prev_v, hl_v, hr_v,
    ao_v, x_v, u_v,
    load_sem, hs_l, hs_r, hr_l, hr_r, cm_s, cm_r, cx_s, cx_r, wf_s, wf_r, we_s, we_r, a_s, a_r,
    f_s, f_r, b_s, b_r, o_s, o_r,
):
    blocks = pat_ref.shape[-1]
    no = inv_v.shape[-1]
    nb = no // blocks
    width = src_v.shape[2] // PARTS
    pos = lax.axis_index("cuts")
    e = lax.axis_index("energy")
    core = lax.rem(e, 2)
    first_e = e - core
    last = cuts - 1
    place = lax.rem(pos, SPAN)
    base = pos - place
    xs = energies // SPAN
    stride = xs
    x = lax.div(e, stride)

    def rows(c):
        return pl.ds(c * width, width)

    def remote(src, dst, send, recv, device):
        return pltpu.make_async_remote_copy(
            src_ref=src, dst_ref=dst, send_sem=send, recv_sem=recv,
            device_id=device, device_id_type=MESH,
        )

    load_cpl = pltpu.make_async_copy(cpl_ref.at[:, 0], cpl_v, load_sem.at[0])
    load_inv = [
        pltpu.make_async_copy(inv_ref.at[:, l, 0], inv_v.at[l], load_sem.at[1 + l]) for l in range(2)
    ]
    load_src = pltpu.make_async_copy(src_ref.at[:, :, 0], src_v, load_sem.at[3])
    load_prev = pltpu.make_async_copy(prev_ref.at[:, :, 0], prev_v, load_sem.at[4])
    load_cpl.start()
    for copy in load_inv:
        copy.start()
    load_src.start()
    load_prev.start()

    def x_peer(step):
        return {"energy": lax.rem(x + step, SPAN) * stride + lax.rem(e, stride)}

    barrier = pltpu.get_barrier_semaphore()
    always = pos >= 0
    partners = [(always, {"energy": first_e + 1 - core})]
    for step in range(1, SPAN):
        there = base + lax.rem(place + step, SPAN)
        partners.append((always, {"cuts": there, "energy": first_e}))
        partners.append((always, {"cuts": there, "energy": first_e + 1}))
        partners.append((always, x_peer(step)))
    partners += [
        ((place == 0) & (pos > 0), {"cuts": pos - 1}),
        ((place == SPAN - 1) & (pos < last), {"cuts": pos + 1}),
        (pos >= SPAN, {"cuts": pos - SPAN}),
        (pos < cuts - SPAN, {"cuts": pos + SPAN}),
        ((core == 0) & (e > 0), {"energy": e - 1}),
        ((core == 1) & (e < energies - 1), {"energy": e + 1}),
    ]
    for there, device in partners:
        @pl.when(there)
        def _():
            pl.semaphore_signal(barrier, inc=1, device_id=device, device_id_type=MESH)
    pl.semaphore_wait(barrier, sum(jnp.where(there, 1, 0) for there, _ in partners))

    def halo_right(c):
        return remote(prev_ref.at[:, :, 0, rows(c)], hl_v.at[:, :, rows(c)], hs_r.at[c], hr_l.at[c], {"energy": e + 1})

    def halo_left(c):
        return remote(prev_ref.at[:, :, 0, rows(c)], hr_v.at[:, :, rows(c)], hs_l.at[c], hr_r.at[c], {"energy": e - 1})

    for c in range(PARTS):
        @pl.when(e < energies - 1)
        def _():
            halo_right(c).start()

        @pl.when(e > 0)
        def _():
            halo_left(c).start()

    load_cpl.wait()
    for a in range(blocks):
        for b in range(blocks):
            keep = pat_ref[0, a, b].astype(F32)
            lanes = slice(b * nb, (b + 1) * nb)
            real = cpl_v[0, a * nb:(a + 1) * nb, lanes].astype(F32)
            imag = cpl_v[1, a * nb:(a + 1) * nb, lanes].astype(F32)
            cm_v[a, :nb, lanes] = (real * (-keep)).astype(BF16)
            cm_v[a, nb:, lanes] = (imag * keep).astype(BF16)

    send_cm = remote(cm_v.at[x], cm1_v.at[x], cm_s, cm_r, {"cuts": pos - 1})

    def share_cm(step):
        return remote(cm1_v.at[x], cm1_v.at[x], cx_s.at[step - 1], cx_r.at[step - 1], x_peer(step))

    def shared_cm(step):
        slot = lax.rem(x + SPAN - step, SPAN)
        return remote(cm1_v.at[slot], cm1_v.at[slot], cx_s.at[step - 1], cx_r.at[step - 1], x_peer(step))

    @pl.when(pos > 0)
    def _():
        send_cm.start()

    for l in range(2):
        load_inv[l].wait()
        it_v[l, :, :no] = inv_v[l, 0].T
        it_v[l, :, no:] = inv_v[l, 1].T

    def product_into(left, l, target):
        @pl.loop(0, blocks)
        def _(t):
            product = jnp.dot(left[t], it_v[l], preferred_element_type=F32)
            real, imag = combined(product)
            top = pl.ds(pl.multiple_of(t * nb, nb), nb)
            target[l, top, :no] = real.astype(BF16)
            target[l, top, no:] = imag.astype(BF16)

    def owner(l):
        return {"cuts": base + 2 * core + l, "energy": first_e + 1}

    def is_owner(l):
        return (core == 1) & (place == 2 + l)

    def hand(src, dst, l, send, recv):
        @pl.when(is_owner(l))
        def _():
            pltpu.make_async_copy(src, dst, recv).start()

        @pl.when(jnp.logical_not(is_owner(l)))
        def _():
            remote(src, dst, send, recv, owner(l)).start()

    def handed(src, dst, l, send, recv):
        @pl.when(jnp.logical_not(is_owner(l)))
        def _():
            remote(src, dst, send, recv, owner(l)).wait_send()

    def wf_args(l):
        return wfo_v.at[l], wf_v.at[place], l, wf_s.at[l], wf_r.at[place]

    def we_args(l):
        return weo_v.at[l], we_v.at[place], l, we_s.at[l], we_r.at[place]

    def a_args(c, l):
        return ao_v.at[c, l], x_v.at[c, 1 + place], l, a_s.at[2 * c + l], a_r.at[PARTS * place + c]

    @pl.when(pos > 0)
    def _():
        for t in range(blocks):
            lanes = slice(t * nb, (t + 1) * nb)
            real = cm_v[t, :nb, :].T
            imag = -(cm_v[t, nb:, :].T)
            for s in range(blocks):
                cmt_v[s, :nb, lanes] = real[s * nb:(s + 1) * nb]
                cmt_v[s, nb:, lanes] = imag[s * nb:(s + 1) * nb]

        @pl.loop(0, 2)
        def _(l):
            product_into(cmt_v, l, wfo_v)
            hand(*wf_args(l))

    @pl.when(pos < last)
    def _():
        send_cm.wait_recv()
        for step in range(1, SPAN):
            share_cm(step).start()

    near = F32(0)
    far = F32(0)
    for mode in range(off_ref.shape[0]):
        near = near + jnp.where(off_ref[mode] == 1, str_ref[mode], F32(0))
        far = far + jnp.where(off_ref[mode] == 2, str_ref[mode], F32(0))
    load_src.wait()
    load_prev.wait()

    @pl.when(e == 0)
    def _():
        hl_v[...] = jnp.zeros(hl_v.shape, BF16)

    @pl.when(e == energies - 1)
    def _():
        hr_v[...] = jnp.zeros(hr_v.shape, BF16)

    for c in range(PARTS):
        at = rows(c)

        @pl.when(e > 0)
        def _():
            halo_right(c).wait_recv()

        @pl.when(e < energies - 1)
        def _():
            halo_left(c).wait_recv()

        own = [prev_v[:, l, at, :].astype(F32) for l in range(2)]
        lo = [hl_v[:, l, at, :].astype(F32) for l in range(2)]
        hi = [hr_v[:, l, at, :].astype(F32) for l in range(2)]
        drives = (
            src_v[:, 0, at, :].astype(F32) + near * (own[1] + lo[1]) + far * (hi[0] + lo[0]),
            src_v[:, 1, at, :].astype(F32) + near * (hi[0] + own[0]) + far * (hi[1] + lo[1]),
        )
        for l in range(2):
            left = drives[l].astype(BF16).reshape(2 * width, no)
            real, imag = combined(jnp.dot(left, it_v[l], preferred_element_type=F32))
            ao_v[c, l, 0] = real.astype(BF16)
            ao_v[c, l, 1] = imag.astype(BF16)
            hand(*a_args(c, l))

    @pl.when(pos < last)
    def _():
        for step in range(1, SPAN):
            shared_cm(step).wait_recv()

        @pl.loop(0, 2)
        def _(l):
            product_into(cm1_v, l, weo_v)

    @pl.when(pos > 0)
    def _():
        for l in range(2):
            handed(*wf_args(l))

    @pl.when(pos < last)
    def _():
        for l in range(2):
            hand(*we_args(l))

    def stepped(given, weights, added):
        left = given[...].reshape(2 * width, no)
        real, imag = combined(jnp.dot(left, weights[...], preferred_element_type=F32))
        return (real + added[0].astype(F32)).astype(BF16), (imag + added[1].astype(F32)).astype(BF16)

    def send_forward(c):
        return remote(x_v.at[c, SPAN], x_v.at[c, 0], f_s.at[c], f_r.at[c], {"cuts": pos + SPAN})

    def send_backward(c):
        return remote(u_v.at[c, 0], u_v.at[c, SPAN], b_s.at[c], b_r.at[c], {"cuts": pos - SPAN})

    def out_at(c, l):
        return out_ref.at[:, l, 0, rows(c)]

    def is_home(j):
        return (place >= 2) & (j == place)

    def out_far(c, j, l):
        device = {"cuts": base + j, "energy": first_e + lax.div(place, 2)}
        return remote(u_v.at[c, j], out_at(c, l), o_s.at[SPAN * c + j], o_r.at[2 * c + l], device)

    def out_here(c, j, l):
        return pltpu.make_async_copy(u_v.at[c, j], out_at(c, l), o_r.at[2 * c + l])

    half_place = lax.rem(place, 2)

    @pl.when(core == 1)
    def _():
        for c in range(PARTS):
            @pl.loop(0, SPAN)
            def _(j):
                remote(ao_v.at[c, 0], x_v.at[c, 1 + j], a_s.at[0], a_r.at[PARTS * j + c], owner(0)).wait_recv()

                @pl.when((j == 0) & (base > 0))
                def _():
                    send_forward(c).wait_recv()

                @pl.when(base + j > 0)
                def _():
                    if c == 0:
                        remote(wfo_v.at[0], wf_v.at[j], wf_s.at[0], wf_r.at[j], owner(0)).wait_recv()
                    here = x_v.at[c, 1 + j]
                    here[0], here[1] = stepped(x_v.at[c, j], wf_v.at[j], here)

            @pl.when(base < cuts - SPAN)
            def _():
                send_forward(c).start()

        for c in range(PARTS):
            @pl.loop(0, SPAN)
            def _(back):
                j = SPAN - 1 - back

                @pl.when((back == 0) & (base < cuts - SPAN))
                def _():
                    send_backward(c).wait_recv()

                @pl.when(base + j < last)
                def _():
                    if c == 0:
                        remote(weo_v.at[0], we_v.at[j], we_s.at[0], we_r.at[j], owner(0)).wait_recv()
                    here = u_v.at[c, j]
                    here[0], here[1] = stepped(u_v.at[c, j + 1], we_v.at[j], x_v.at[c, 1 + j])

                @pl.when(base + j == last)
                def _():
                    u_v[c, j] = x_v[c, 1 + j]

                @pl.when((j == 0) & (base > 0))
                def _():
                    send_backward(c).start()

                for l in range(2):
                    @pl.when((half_place == l) & is_home(j))
                    def _():
                        out_here(c, j, l).start()

                    @pl.when((half_place == l) & jnp.logical_not(is_home(j)))
                    def _():
                        out_far(c, j, l).start()

    for c in range(PARTS):
        for l in range(2):
            out_far(c, 0, l).wait_recv()
            handed(*a_args(c, l))

        @pl.when(core == 1)
        def _():
            @pl.loop(0, SPAN)
            def _(j):
                @pl.when(jnp.logical_not(is_home(j)))
                def _():
                    out_far(c, j, 0).wait_send()

            @pl.when(base < cuts - SPAN)
            def _():
                send_forward(c).wait_send()

            @pl.when(base > 0)
            def _():
                send_backward(c).wait_send()

        @pl.when(e < energies - 1)
        def _():
            halo_right(c).wait_send()

        @pl.when(e > 0)
        def _():
            halo_left(c).wait_send()

    @pl.when(pos > 0)
    def _():
        send_cm.wait_send()

    @pl.when(pos < last)
    def _():
        for step in range(1, SPAN):
            share_cm(step).wait_send()
        for l in range(2):
            handed(*we_args(l))


def on_device(cuts, energies, inverse, coupling, pattern, source, previous, offsets, strength):
    no, nr = source.shape[4], source.shape[3]
    blocks = pattern.shape[-1]
    width = nr // PARTS
    dma = pltpu.SemaphoreType.DMA
    panel = pltpu.VMEM((2, 2, nr, no), BF16)
    stack = pltpu.VMEM((blocks, 2 * no // blocks, no), BF16)
    anywhere = pl.BlockSpec(memory_space=pl.ANY)
    scalars = pl.BlockSpec(memory_space=pltpu.SMEM)
    return pl.pallas_call(
        functools.partial(sweep_kernel, cuts, energies),
        name="sweeps",
        out_shape=jax.ShapeDtypeStruct(source.shape, BF16),
        in_specs=[anywhere, anywhere, scalars, anywhere, anywhere, scalars, scalars],
        out_specs=anywhere,
        scratch_shapes=[
            pltpu.VMEM((2, 2, no, no), BF16),
            pltpu.VMEM((2, no, 2 * no), BF16),
            pltpu.VMEM((2, no, no), BF16),
            stack, stack, stack,
            pltpu.VMEM((2, no, 2 * no), BF16),
            pltpu.VMEM((2, no, 2 * no), BF16),
            pltpu.VMEM((SPAN, no, 2 * no), BF16),
            pltpu.VMEM((SPAN, no, 2 * no), BF16),
            panel, panel, panel, panel,
            pltpu.VMEM((PARTS, 2, 2, width, no), BF16),
            pltpu.VMEM((PARTS, SPAN + 1, 2, width, no), BF16),
            pltpu.VMEM((PARTS, SPAN + 1, 2, width, no), BF16),
            dma((5,)),
            dma((PARTS,)), dma((PARTS,)), dma((PARTS,)), dma((PARTS,)),
            dma, dma,
            dma((SPAN - 1,)), dma((SPAN - 1,)),
            dma((2,)), dma((SPAN,)), dma((2,)), dma((SPAN,)),
            dma((2 * PARTS,)), dma((SPAN * PARTS,)),
            dma((PARTS,)), dma((PARTS,)), dma((PARTS,)), dma((PARTS,)),
            dma((SPAN * PARTS,)), dma((2 * PARTS,)),
        ],
        compiler_params=pltpu.CompilerParams(
            collective_id=0, has_side_effects=True, vmem_limit_bytes=60 << 20
        ),
    )(inverse, coupling, pattern, source, previous, offsets, strength)


def solution(mesh):
    return jax.shard_map(
        functools.partial(on_device, mesh.shape["cuts"], mesh.shape["energy"]),
        mesh=mesh,
        in_specs=(
            P(None, "energy", "cuts", None, None),
            P(None, "cuts", None, None),
            P("cuts", None, None),
            P(None, "energy", "cuts", None, None),
            P(None, "energy", "cuts", None, None),
            P(),
            P(),
        ),
        out_specs=P(None, "energy", "cuts", None, None),
        check_vma=False,
    )
```

```python
import functools

import jax
import jax.numpy as jnp
from jax import lax
from jax.experimental import pallas as pl
from jax.experimental.pallas import tpu as pltpu
from jax.sharding import PartitionSpec as P

MESH = pl.DeviceIdType.MESH
F32 = jnp.float32
BF16 = jnp.bfloat16
SPAN = 4
PARTS = 2


def combined(product):
    h, w = product.shape[0] // 2, product.shape[1] // 2
    real = product[:h, :w] - product[h:, w:]
    imag = product[:h, w:] + product[h:, :w]
    return real, imag


def sweep_kernel(
    cuts, energies, inv_ref, cpl_ref, pat_ref, src_ref, prev_ref, off_ref, str_ref, out_ref,
    inv_v, it_v, cpl_v, cm_v, cmt_v, cm1_v, wfo_v, weo_v, wf_v, we_v, src_v, prev_v, hl_v, hr_v,
    ao_v, x_v, u_v,
    load_sem, hs_l, hs_r, hr_l, hr_r, cm_s, cm_r, cx_s, cx_r, cc_s, cc_r, wf_s, wf_r, we_s, we_r, a_s, a_r,
    f_s, f_r, b_s, b_r, o_s, o_r,
):
    blocks = pat_ref.shape[-1]
    no = inv_v.shape[-1]
    nb = no // blocks
    width = src_v.shape[2] // PARTS
    pos = lax.axis_index("cuts")
    e = lax.axis_index("energy")
    core = lax.rem(e, 2)
    first_e = e - core
    last = cuts - 1
    place = lax.rem(pos, SPAN)
    base = pos - place
    xs = energies // SPAN
    stride = xs
    x = lax.div(e, stride)

    def rows(c):
        return pl.ds(c * width, width)

    def remote(src, dst, send, recv, device):
        return pltpu.make_async_remote_copy(
            src_ref=src, dst_ref=dst, send_sem=send, recv_sem=recv,
            device_id=device, device_id_type=MESH,
        )

    load_cpl = pltpu.make_async_copy(cpl_ref.at[:, 0], cpl_v, load_sem.at[0])
    load_inv = [
        pltpu.make_async_copy(inv_ref.at[:, l, 0], inv_v.at[l], load_sem.at[1 + l]) for l in range(2)
    ]
    load_src = pltpu.make_async_copy(src_ref.at[:, :, 0], src_v, load_sem.at[3])
    load_prev = pltpu.make_async_copy(prev_ref.at[:, :, 0], prev_v, load_sem.at[4])
    load_cpl.start()
    for copy in load_inv:
        copy.start()
    load_src.start()
    load_prev.start()

    def x_peer(step):
        return {"energy": lax.rem(x + step, SPAN) * stride + lax.rem(e, stride)}

    barrier = pltpu.get_barrier_semaphore()
    always = pos >= 0
    partners = [(always, {"energy": first_e + 1 - core})]
    for step in range(1, SPAN):
        there = base + lax.rem(place + step, SPAN)
        partners.append((always, {"cuts": there, "energy": first_e}))
        partners.append((always, {"cuts": there, "energy": first_e + 1}))
        partners.append((always, x_peer(step)))
    partners += [
        ((place == 0) & (pos > 0), {"cuts": pos - 1}),
        ((place == SPAN - 1) & (pos < last), {"cuts": pos + 1}),
        (pos >= SPAN, {"cuts": pos - SPAN}),
        (pos < cuts - SPAN, {"cuts": pos + SPAN}),
        ((core == 0) & (e > 0), {"energy": e - 1}),
        ((core == 1) & (e < energies - 1), {"energy": e + 1}),
    ]
    for there, device in partners:
        @pl.when(there)
        def _():
            pl.semaphore_signal(barrier, inc=1, device_id=device, device_id_type=MESH)

    def halo_right(c):
        return remote(prev_ref.at[:, :, 0, rows(c)], hl_v.at[:, :, rows(c)], hs_r.at[c], hr_l.at[c], {"energy": e + 1})

    def halo_left(c):
        return remote(prev_ref.at[:, :, 0, rows(c)], hr_v.at[:, :, rows(c)], hs_l.at[c], hr_r.at[c], {"energy": e - 1})

    load_cpl.wait()
    for a in range(blocks):
        for b in range(blocks):
            keep = pat_ref[0, a, b].astype(F32)
            lanes = slice(b * nb, (b + 1) * nb)
            real = cpl_v[0, a * nb:(a + 1) * nb, lanes].astype(F32)
            imag = cpl_v[1, a * nb:(a + 1) * nb, lanes].astype(F32)
            cm_v[a, :nb, lanes] = (real * (-keep)).astype(BF16)
            cm_v[a, nb:, lanes] = (imag * keep).astype(BF16)

    half = pl.ds(pl.multiple_of(core * nb, nb), nb)
    send_cm = remote(cm_v.at[x, half], cm1_v.at[x, half], cm_s, cm_r, {"cuts": pos - 1})

    def share_cm(step):
        return remote(cm1_v.at[x, half], cm1_v.at[x, half], cx_s.at[step - 1], cx_r.at[step - 1], x_peer(step))

    def shared_cm(step):
        slot = lax.rem(x + SPAN - step, SPAN)
        return remote(
            cm1_v.at[slot, half], cm1_v.at[slot, half], cx_s.at[step - 1], cx_r.at[step - 1], x_peer(step)
        )

    mate_cm = remote(cm1_v.at[:, half], cm1_v.at[:, half], cc_s, cc_r, {"energy": first_e + 1 - core})

    def pool_cm():
        for step in range(1, SPAN):
            shared_cm(step).wait_recv()
        mate_cm.start()

    for l in range(2):
        load_inv[l].wait()
        it_v[l, :, :no] = inv_v[l, 0].T
        it_v[l, :, no:] = inv_v[l, 1].T

    def product_into(left, l, target):
        product = jnp.dot(left[...].reshape(2 * no, no), it_v[l], preferred_element_type=F32)
        for t in range(blocks):
            real, imag = combined(product[2 * nb * t:2 * nb * (t + 1)])
            target[l, nb * t:nb * (t + 1), :no] = real.astype(BF16)
            target[l, nb * t:nb * (t + 1), no:] = imag.astype(BF16)

    def owner(l):
        return {"cuts": base + 2 * core + l, "energy": first_e + 1}

    def is_owner(l):
        return (core == 1) & (place == 2 + l)

    def hand(src, dst, l, send, recv):
        @pl.when(is_owner(l))
        def _():
            pltpu.make_async_copy(src, dst, recv).start()

        @pl.when(jnp.logical_not(is_owner(l)))
        def _():
            remote(src, dst, send, recv, owner(l)).start()

    def handed(src, dst, l, send, recv):
        @pl.when(jnp.logical_not(is_owner(l)))
        def _():
            remote(src, dst, send, recv, owner(l)).wait_send()

    def wf_args(l):
        return wfo_v.at[l], wf_v.at[place], l, wf_s.at[l], wf_r.at[place]

    def we_args(l):
        return weo_v.at[l], we_v.at[place], l, we_s.at[l], we_r.at[place]

    def a_args(c, l):
        return ao_v.at[c, l], x_v.at[c, 1 + place], l, a_s.at[2 * c + l], a_r.at[PARTS * place + c]

    @pl.when(pos > 0)
    def _():
        for t in range(blocks):
            lanes = slice(t * nb, (t + 1) * nb)
            real = cm_v[t, :nb, :].T
            imag = -(cm_v[t, nb:, :].T)
            for s in range(blocks):
                cmt_v[s, :nb, lanes] = real[s * nb:(s + 1) * nb]
                cmt_v[s, nb:, lanes] = imag[s * nb:(s + 1) * nb]

        @pl.loop(0, 2)
        def _(l):
            product_into(cmt_v, l, wfo_v)

    pl.semaphore_wait(barrier, sum(jnp.where(there, 1, 0) for there, _ in partners))

    @pl.when(pos > 0)
    def _():
        send_cm.start()

    for c in range(PARTS):
        @pl.when(e < energies - 1)
        def _():
            halo_right(c).start()

        @pl.when(e > 0)
        def _():
            halo_left(c).start()

    @pl.when(pos > 0)
    def _():
        for l in range(2):
            hand(*wf_args(l))

    @pl.when(pos < last)
    def _():
        send_cm.wait_recv()
        for step in range(1, SPAN):
            share_cm(step).start()

    @pl.when((pos < last) & (place < SPAN - 1))
    def _():
        pool_cm()

    near = F32(0)
    far = F32(0)
    for mode in range(off_ref.shape[0]):
        near = near + jnp.where(off_ref[mode] == 1, str_ref[mode], F32(0))
        far = far + jnp.where(off_ref[mode] == 2, str_ref[mode], F32(0))
    load_src.wait()
    load_prev.wait()

    @pl.when(e == 0)
    def _():
        hl_v[...] = jnp.zeros(hl_v.shape, BF16)

    @pl.when(e == energies - 1)
    def _():
        hr_v[...] = jnp.zeros(hr_v.shape, BF16)

    for c in range(PARTS):
        at = rows(c)

        @pl.when(e > 0)
        def _():
            halo_right(c).wait_recv()

        @pl.when(e < energies - 1)
        def _():
            halo_left(c).wait_recv()

        own = [prev_v[:, l, at, :].astype(F32) for l in range(2)]
        lo = [hl_v[:, l, at, :].astype(F32) for l in range(2)]
        hi = [hr_v[:, l, at, :].astype(F32) for l in range(2)]
        drives = (
            src_v[:, 0, at, :].astype(F32) + near * (own[1] + lo[1]) + far * (hi[0] + lo[0]),
            src_v[:, 1, at, :].astype(F32) + near * (hi[0] + own[0]) + far * (hi[1] + lo[1]),
        )
        for l in range(2):
            left = drives[l].astype(BF16).reshape(2 * width, no)
            real, imag = combined(jnp.dot(left, it_v[l], preferred_element_type=F32))
            ao_v[c, l, 0] = real.astype(BF16)
            ao_v[c, l, 1] = imag.astype(BF16)
            hand(*a_args(c, l))

    @pl.when((pos < last) & (place == SPAN - 1))
    def _():
        pool_cm()

    @pl.when(pos < last)
    def _():
        mate_cm.wait_recv()

        @pl.loop(0, 2)
        def _(l):
            product_into(cm1_v, l, weo_v)

    @pl.when(pos > 0)
    def _():
        for l in range(2):
            handed(*wf_args(l))

    @pl.when(pos < last)
    def _():
        for l in range(2):
            hand(*we_args(l))

    def stepped(given, weights, added):
        left = given[...].reshape(2 * width, no)
        real, imag = combined(jnp.dot(left, weights[...], preferred_element_type=F32))
        return (real + added[0].astype(F32)).astype(BF16), (imag + added[1].astype(F32)).astype(BF16)

    def send_forward(c):
        return remote(x_v.at[c, SPAN], x_v.at[c, 0], f_s.at[c], f_r.at[c], {"cuts": pos + SPAN})

    def send_backward(c):
        return remote(u_v.at[c, 0], u_v.at[c, SPAN], b_s.at[c], b_r.at[c], {"cuts": pos - SPAN})

    def out_at(c, l):
        return out_ref.at[:, l, 0, rows(c)]

    def is_home(j):
        return (place >= 2) & (j == place)

    def out_far(c, j, l):
        device = {"cuts": base + j, "energy": first_e + lax.div(place, 2)}
        return remote(u_v.at[c, j], out_at(c, l), o_s.at[SPAN * c + j], o_r.at[2 * c + l], device)

    def out_here(c, j, l):
        return pltpu.make_async_copy(u_v.at[c, j], out_at(c, l), o_r.at[2 * c + l])

    half_place = lax.rem(place, 2)

    @pl.when(core == 1)
    def _():
        for c in range(PARTS):
            @pl.loop(0, SPAN)
            def _(j):
                remote(ao_v.at[c, 0], x_v.at[c, 1 + j], a_s.at[0], a_r.at[PARTS * j + c], owner(0)).wait_recv()

                @pl.when((j == 0) & (base > 0))
                def _():
                    send_forward(c).wait_recv()

                @pl.when(base + j > 0)
                def _():
                    if c == 0:
                        remote(wfo_v.at[0], wf_v.at[j], wf_s.at[0], wf_r.at[j], owner(0)).wait_recv()
                    here = x_v.at[c, 1 + j]
                    here[0], here[1] = stepped(x_v.at[c, j], wf_v.at[j], here)

            @pl.when(base < cuts - SPAN)
            def _():
                send_forward(c).start()

        for c in range(PARTS):
            @pl.loop(0, SPAN)
            def _(back):
                j = SPAN - 1 - back

                @pl.when((back == 0) & (base < cuts - SPAN))
                def _():
                    send_backward(c).wait_recv()

                @pl.when(base + j < last)
                def _():
                    if c == 0:
                        remote(weo_v.at[0], we_v.at[j], we_s.at[0], we_r.at[j], owner(0)).wait_recv()
                    here = u_v.at[c, j]
                    here[0], here[1] = stepped(u_v.at[c, j + 1], we_v.at[j], x_v.at[c, 1 + j])

                @pl.when(base + j == last)
                def _():
                    u_v[c, j] = x_v[c, 1 + j]

                @pl.when((j == 0) & (base > 0))
                def _():
                    send_backward(c).start()

                for l in range(2):
                    @pl.when((half_place == l) & is_home(j))
                    def _():
                        out_here(c, j, l).start()

                    @pl.when((half_place == l) & jnp.logical_not(is_home(j)))
                    def _():
                        out_far(c, j, l).start()

    for c in range(PARTS):
        for l in range(2):
            out_far(c, 0, l).wait_recv()
            handed(*a_args(c, l))

        @pl.when(core == 1)
        def _():
            @pl.loop(0, SPAN)
            def _(j):
                @pl.when(jnp.logical_not(is_home(j)))
                def _():
                    out_far(c, j, 0).wait_send()

            @pl.when(base < cuts - SPAN)
            def _():
                send_forward(c).wait_send()

            @pl.when(base > 0)
            def _():
                send_backward(c).wait_send()

        @pl.when(e < energies - 1)
        def _():
            halo_right(c).wait_send()

        @pl.when(e > 0)
        def _():
            halo_left(c).wait_send()

    @pl.when(pos > 0)
    def _():
        send_cm.wait_send()

    @pl.when(pos < last)
    def _():
        for step in range(1, SPAN):
            share_cm(step).wait_send()
        mate_cm.wait_send()
        for l in range(2):
            handed(*we_args(l))


def on_device(cuts, energies, inverse, coupling, pattern, source, previous, offsets, strength):
    no, nr = source.shape[4], source.shape[3]
    blocks = pattern.shape[-1]
    width = nr // PARTS
    dma = pltpu.SemaphoreType.DMA
    panel = pltpu.VMEM((2, 2, nr, no), BF16)
    stack = pltpu.VMEM((blocks, 2 * no // blocks, no), BF16)
    anywhere = pl.BlockSpec(memory_space=pl.ANY)
    scalars = pl.BlockSpec(memory_space=pltpu.SMEM)
    return pl.pallas_call(
        functools.partial(sweep_kernel, cuts, energies),
        name="sweeps",
        out_shape=jax.ShapeDtypeStruct(source.shape, BF16),
        in_specs=[anywhere, anywhere, scalars, anywhere, anywhere, scalars, scalars],
        out_specs=anywhere,
        scratch_shapes=[
            pltpu.VMEM((2, 2, no, no), BF16),
            pltpu.VMEM((2, no, 2 * no), BF16),
            pltpu.VMEM((2, no, no), BF16),
            stack, stack, stack,
            pltpu.VMEM((2, no, 2 * no), BF16),
            pltpu.VMEM((2, no, 2 * no), BF16),
            pltpu.VMEM((SPAN, no, 2 * no), BF16),
            pltpu.VMEM((SPAN, no, 2 * no), BF16),
            panel, panel, panel, panel,
            pltpu.VMEM((PARTS, 2, 2, width, no), BF16),
            pltpu.VMEM((PARTS, SPAN + 1, 2, width, no), BF16),
            pltpu.VMEM((PARTS, SPAN + 1, 2, width, no), BF16),
            dma((5,)),
            dma((PARTS,)), dma((PARTS,)), dma((PARTS,)), dma((PARTS,)),
            dma, dma,
            dma((SPAN - 1,)), dma((SPAN - 1,)),
            dma, dma,
            dma((2,)), dma((SPAN,)), dma((2,)), dma((SPAN,)),
            dma((2 * PARTS,)), dma((SPAN * PARTS,)),
            dma((PARTS,)), dma((PARTS,)), dma((PARTS,)), dma((PARTS,)),
            dma((SPAN * PARTS,)), dma((2 * PARTS,)),
        ],
        compiler_params=pltpu.CompilerParams(
            collective_id=0, has_side_effects=True, vmem_limit_bytes=60 << 20
        ),
    )(inverse, coupling, pattern, source, previous, offsets, strength)


def solution(mesh):
    return jax.shard_map(
        functools.partial(on_device, mesh.shape["cuts"], mesh.shape["energy"]),
        mesh=mesh,
        in_specs=(
            P(None, "energy", "cuts", None, None),
            P(None, "cuts", None, None),
            P("cuts", None, None),
            P(None, "energy", "cuts", None, None),
            P(None, "energy", "cuts", None, None),
            P(),
            P(),
        ),
        out_specs=P(None, "energy", "cuts", None, None),
        check_vma=False,
    )
```

```python
import functools

import jax
import jax.numpy as jnp
from jax import lax
from jax.experimental import pallas as pl
from jax.experimental.pallas import tpu as pltpu
from jax.sharding import PartitionSpec as P

MESH = pl.DeviceIdType.MESH
F32 = jnp.float32
BF16 = jnp.bfloat16
SPAN = 4
PARTS = 2


def combined(product):
    h, w = product.shape[0] // 2, product.shape[1] // 2
    real = product[:h, :w] - product[h:, w:]
    imag = product[:h, w:] + product[h:, :w]
    return real, imag


def sweep_kernel(
    cuts, energies, inv_ref, cpl_ref, pat_ref, src_ref, prev_ref, off_ref, str_ref, out_ref,
    inv_v, it_v, cpl_v, cm_v, cmt_v, cmr_v, wfo_v, weo_v, wf_v, we_v, itr_v, src_v, prev_v, hl_v, hr_v,
    ao_v, x_v, u_v,
    load_sem, hs_l, hs_r, hr_l, hr_r, cm_s, cm_r, ring_s, ring_r, cx_s, cx_r, cc_s, cc_r, fw_s, fw_r, fe_s, wf_s, wf_r, we_s, we_r, a_s, a_r,
    f_s, f_r, b_s, b_r, o_s, o_r,
):
    blocks = pat_ref.shape[-1]
    no = inv_v.shape[-1]
    nb = no // blocks
    width = src_v.shape[2] // PARTS
    pos = lax.axis_index("cuts")
    e = lax.axis_index("energy")
    core = lax.rem(e, 2)
    first_e = e - core
    last = cuts - 1
    place = lax.rem(pos, SPAN)
    base = pos - place
    stride = energies // SPAN
    x = lax.div(e, stride)
    late = base >= cuts // 2
    early = base < cuts // 2
    final_group = base == cuts - SPAN

    def rows(c):
        return pl.ds(c * width, width)

    def remote(src, dst, send, recv, device):
        return pltpu.make_async_remote_copy(
            src_ref=src, dst_ref=dst, send_sem=send, recv_sem=recv,
            device_id=device, device_id_type=MESH,
        )

    load_cpl = pltpu.make_async_copy(cpl_ref.at[:, 0], cpl_v, load_sem.at[0])
    load_inv = [
        pltpu.make_async_copy(inv_ref.at[:, l, 0], inv_v.at[l], load_sem.at[1 + l]) for l in range(2)
    ]
    load_src = pltpu.make_async_copy(src_ref.at[:, :, 0], src_v, load_sem.at[3])
    load_prev = pltpu.make_async_copy(prev_ref.at[:, :, 0], prev_v, load_sem.at[4])
    load_cpl.start()
    for copy in load_inv:
        copy.start()
    load_src.start()
    load_prev.start()

    def x_peer(step):
        return {"energy": lax.rem(x + step, SPAN) * stride + lax.rem(e, stride)}

    barrier = pltpu.get_barrier_semaphore()
    always = pos >= 0
    partners = [(always, {"energy": first_e + 1 - core})]
    for step in range(1, SPAN):
        there = base + lax.rem(place + step, SPAN)
        partners.append((always, {"cuts": there, "energy": first_e}))
        partners.append((always, {"cuts": there, "energy": first_e + 1}))
        partners.append((always, x_peer(step)))
    partners += [
        ((place == 0) & (pos > 0), {"cuts": pos - 1}),
        ((place == SPAN - 1) & (pos < last), {"cuts": pos + 1}),
        (pos >= SPAN, {"cuts": pos - SPAN}),
        (pos < cuts - SPAN, {"cuts": pos + SPAN}),
        ((core == 0) & (e > 0), {"energy": e - 1}),
        ((core == 1) & (e < energies - 1), {"energy": e + 1}),
    ]
    for there, device in partners:
        @pl.when(there)
        def _():
            pl.semaphore_signal(barrier, inc=1, device_id=device, device_id_type=MESH)

    def halo_right(c):
        return remote(prev_ref.at[:, :, 0, rows(c)], hl_v.at[:, :, rows(c)], hs_r.at[c], hr_l.at[c], {"energy": e + 1})

    def halo_left(c):
        return remote(prev_ref.at[:, :, 0, rows(c)], hr_v.at[:, :, rows(c)], hs_l.at[c], hr_r.at[c], {"energy": e - 1})

    load_cpl.wait()
    for a in range(blocks):
        for b in range(blocks):
            keep = pat_ref[0, a, b].astype(F32)
            lanes = slice(b * nb, (b + 1) * nb)
            real = cpl_v[0, a * nb:(a + 1) * nb, lanes].astype(F32)
            imag = cpl_v[1, a * nb:(a + 1) * nb, lanes].astype(F32)
            cm_v[a, :nb, lanes] = (real * (-keep)).astype(BF16)
            cm_v[a, nb:, lanes] = (imag * keep).astype(BF16)

    half = pl.ds(pl.multiple_of(core * nb, nb), nb)
    send_cm = remote(cm_v.at[x, half], cmr_v.at[SPAN, x, half], cm_s, cm_r, {"cuts": pos - 1})
    shifts_out = (pos > 0) & (pos <= cuts // 2)

    def in_ring(step):
        return {"cuts": base + lax.rem(place + step, SPAN)}

    def ring_cm(step):
        return remote(cm_v.at[x, half], cmr_v.at[place, x, half], ring_s.at[step - 1], ring_r.at[place], in_ring(step))

    def ringed_cm(slot):
        return remote(cm_v.at[x, half], cmr_v.at[slot, x, half], ring_s.at[0], ring_r.at[slot], in_ring(1))

    def share_cm(slot, step):
        piece = cmr_v.at[slot, x, half]
        n = (SPAN - 1) * slot + step - 1
        return remote(piece, piece, cx_s.at[n], cx_r.at[n], x_peer(step))

    def shared_cm(slot, step):
        piece = cmr_v.at[slot, lax.rem(x + SPAN - step, SPAN), half]
        n = (SPAN - 1) * slot + step - 1
        return remote(piece, piece, cx_s.at[n], cx_r.at[n], x_peer(step))

    def mate_cm(slot):
        piece = cmr_v.at[slot, :, half]
        return remote(piece, piece, cc_s.at[slot], cc_r.at[slot], {"energy": first_e + 1 - core})

    def pool_cm(slot):
        for step in range(1, SPAN):
            shared_cm(slot, step).wait_recv()

    for l in range(2):
        load_inv[l].wait()
        it_v[l, :, :no] = inv_v[l, 0].T
        it_v[l, :, no:] = inv_v[l, 1].T

    def product_into(left, right, target):
        product = jnp.dot(left[...].reshape(2 * no, no), right[...], preferred_element_type=F32)
        for t in range(blocks):
            real, imag = combined(product[2 * nb * t:2 * nb * (t + 1)])
            target[nb * t:nb * (t + 1), :no] = real.astype(BF16)
            target[nb * t:nb * (t + 1), no:] = imag.astype(BF16)

    def owner(l):
        return {"cuts": base + 2 * core + l, "energy": first_e + 1}

    def is_owner(l):
        return (core == 1) & (place == 2 + l)

    def hand(src, dst, l, send, recv):
        @pl.when(is_owner(l))
        def _():
            pltpu.make_async_copy(src, dst, recv).start()

        @pl.when(jnp.logical_not(is_owner(l)))
        def _():
            remote(src, dst, send, recv, owner(l)).start()

    def handed(src, dst, l, send, recv):
        @pl.when(jnp.logical_not(is_owner(l)))
        def _():
            remote(src, dst, send, recv, owner(l)).wait_send()

    def wf_args(l):
        return wfo_v.at[l], wf_v.at[place], l, wf_s.at[l], wf_r.at[place]

    def we_args(l):
        return weo_v.at[l], we_v.at[place], l, we_s.at[l], we_r.at[place]

    def it_args(l):
        return it_v.at[l], itr_v.at[place], l, wf_s.at[l], wf_r.at[place]

    def a_args(c, l):
        return ao_v.at[c, l], x_v.at[c, 1 + place], l, a_s.at[2 * c + l], a_r.at[PARTS * place + c]

    def turn(given):
        for t in range(blocks):
            lanes = slice(t * nb, (t + 1) * nb)
            real = given[t, :nb, :].T
            imag = -(given[t, nb:, :].T)
            for s in range(blocks):
                cmt_v[s, :nb, lanes] = real[s * nb:(s + 1) * nb]
                cmt_v[s, nb:, lanes] = imag[s * nb:(s + 1) * nb]

    @pl.when((pos > 0) & early)
    def _():
        turn(cm_v)

        @pl.loop(0, 2)
        def _(l):
            product_into(cmt_v, it_v.at[l], wfo_v.at[l])

    @pl.when(late)
    def _():
        cmr_v[place] = cm_v[...]

    pl.semaphore_wait(barrier, sum(jnp.where(there, 1, 0) for there, _ in partners))

    @pl.when(shifts_out)
    def _():
        send_cm.start()

    @pl.when(late)
    def _():
        for step in range(1, SPAN):
            ring_cm(step).start()

    for c in range(PARTS):
        @pl.when(e < energies - 1)
        def _():
            halo_right(c).start()

        @pl.when(e > 0)
        def _():
            halo_left(c).start()

    @pl.when((pos > 0) & early)
    def _():
        for l in range(2):
            hand(*wf_args(l))

    @pl.when(late)
    def _():
        for slot in range(SPAN):
            @pl.when(slot != place)
            def _():
                ringed_cm(slot).wait_recv()
                for step in range(1, SPAN):
                    share_cm(slot, step).start()
        for l in range(2):
            hand(*it_args(l))

    @pl.when(early)
    def _():
        send_cm.wait_recv()
        for step in range(1, SPAN):
            share_cm(SPAN, step).start()

    @pl.when(early & (place < SPAN - 1))
    def _():
        pool_cm(SPAN)
        mate_cm(SPAN).start()

    near = F32(0)
    far = F32(0)
    for mode in range(off_ref.shape[0]):
        near = near + jnp.where(off_ref[mode] == 1, str_ref[mode], F32(0))
        far = far + jnp.where(off_ref[mode] == 2, str_ref[mode], F32(0))
    load_src.wait()
    load_prev.wait()

    @pl.when(e == 0)
    def _():
        hl_v[...] = jnp.zeros(hl_v.shape, BF16)

    @pl.when(e == energies - 1)
    def _():
        hr_v[...] = jnp.zeros(hr_v.shape, BF16)

    for c in range(PARTS):
        at = rows(c)

        @pl.when(e > 0)
        def _():
            halo_right(c).wait_recv()

        @pl.when(e < energies - 1)
        def _():
            halo_left(c).wait_recv()

        own = [prev_v[:, l, at, :].astype(F32) for l in range(2)]
        lo = [hl_v[:, l, at, :].astype(F32) for l in range(2)]
        hi = [hr_v[:, l, at, :].astype(F32) for l in range(2)]
        drives = (
            src_v[:, 0, at, :].astype(F32) + near * (own[1] + lo[1]) + far * (hi[0] + lo[0]),
            src_v[:, 1, at, :].astype(F32) + near * (hi[0] + own[0]) + far * (hi[1] + lo[1]),
        )
        for l in range(2):
            left = drives[l].astype(BF16).reshape(2 * width, no)
            real, imag = combined(jnp.dot(left, it_v[l], preferred_element_type=F32))
            ao_v[c, l, 0] = real.astype(BF16)
            ao_v[c, l, 1] = imag.astype(BF16)
            hand(*a_args(c, l))

    @pl.when(early & (place == SPAN - 1))
    def _():
        pool_cm(SPAN)
        mate_cm(SPAN).start()

    @pl.when(early)
    def _():
        mate_cm(SPAN).wait_recv()

        @pl.loop(0, 2)
        def _(l):
            product_into(cmr_v.at[SPAN], it_v.at[l], weo_v.at[l])

    @pl.when((pos > 0) & early)
    def _():
        for l in range(2):
            handed(*wf_args(l))

    @pl.when(early)
    def _():
        for l in range(2):
            hand(*we_args(l))

    @pl.when(late)
    def _():
        for slot in range(SPAN):
            @pl.when(slot != place)
            def _():
                pool_cm(slot)
                mate_cm(slot).start()

        for slot in range(SPAN):
            @pl.when(slot != place)
            def _():
                mate_cm(slot).wait_recv()

    def pass_on(j):
        return remote(itr_v.at[j], itr_v.at[j], fw_s.at[j], fw_r.at[j], {"energy": first_e + 1 - core})

    def pass_back(j):
        return remote(we_v.at[j], we_v.at[j], fe_s.at[j], we_r.at[j], {"energy": first_e + 1 - core})

    @pl.when(late & (core == 1))
    def _():
        @pl.loop(0, SPAN)
        def _(back):
            j = SPAN - 1 - back
            remote(it_v.at[0], itr_v.at[j], wf_s.at[0], wf_r.at[j], owner(0)).wait_recv()

            @pl.when(j < SPAN - 1)
            def _():
                pass_on(j).start()

        @pl.loop(0, SPAN)
        def _(j):
            turn(cmr_v.at[j])
            product_into(cmt_v, itr_v.at[j], wf_v.at[j])

        @pl.when(final_group)
        def _():
            for t in range(blocks):
                we_v[SPAN - 1, nb * t:nb * (t + 1), :no] = cmr_v[0, t, :nb]
                we_v[SPAN - 1, nb * t:nb * (t + 1), no:] = cmr_v[0, t, nb:]

        @pl.when(jnp.logical_not(final_group))
        def _():
            we_v[SPAN - 1] = itr_v[SPAN - 1]

    @pl.when(late & (core == 0))
    def _():
        @pl.loop(0, SPAN - 1)
        def _(back):
            j = SPAN - 2 - back
            pass_on(j).wait_recv()
            product_into(cmr_v.at[j + 1], itr_v.at[j], we_v.at[j])
            pass_back(j).start()

    def stepped(given, weights, added):
        left = given[...].reshape(2 * width, no)
        real, imag = combined(jnp.dot(left, weights[...], preferred_element_type=F32))
        return (real + added[0].astype(F32)).astype(BF16), (imag + added[1].astype(F32)).astype(BF16)

    def send_forward(c):
        return remote(x_v.at[c, SPAN], x_v.at[c, 0], f_s.at[c], f_r.at[c], {"cuts": pos + SPAN})

    def send_backward(c):
        return remote(u_v.at[c, 0], u_v.at[c, SPAN], b_s.at[c], b_r.at[c], {"cuts": pos - SPAN})

    def send_coupled(c):
        return remote(x_v.at[c, 0], u_v.at[c, SPAN], b_s.at[c], b_r.at[c], {"cuts": pos - SPAN})

    def out_at(c, l):
        return out_ref.at[:, l, 0, rows(c)]

    def is_home(j):
        return (place >= 2) & (j == place)

    def out_far(c, j, l):
        device = {"cuts": base + j, "energy": first_e + lax.div(place, 2)}
        return remote(u_v.at[c, j], out_at(c, l), o_s.at[SPAN * c + j], o_r.at[2 * c + l], device)

    def out_here(c, j, l):
        return pltpu.make_async_copy(u_v.at[c, j], out_at(c, l), o_r.at[2 * c + l])

    half_place = lax.rem(place, 2)

    @pl.when(core == 1)
    def _():
        for c in range(PARTS):
            @pl.loop(0, SPAN)
            def _(j):
                remote(ao_v.at[c, 0], x_v.at[c, 1 + j], a_s.at[0], a_r.at[PARTS * j + c], owner(0)).wait_recv()

                @pl.when((j == 0) & (base > 0))
                def _():
                    send_forward(c).wait_recv()

                @pl.when(base + j > 0)
                def _():
                    if c == 0:
                        @pl.when(early)
                        def _():
                            remote(wfo_v.at[0], wf_v.at[j], wf_s.at[0], wf_r.at[j], owner(0)).wait_recv()

                    here = x_v.at[c, 1 + j]
                    here[0], here[1] = stepped(x_v.at[c, j], wf_v.at[j], here)

            @pl.when(base < cuts - SPAN)
            def _():
                send_forward(c).start()

        for c in range(PARTS):
            @pl.loop(0, SPAN)
            def _(back):
                j = SPAN - 1 - back

                @pl.when((back == 0) & (base < cuts - SPAN))
                def _():
                    send_backward(c).wait_recv()

                @pl.when(base + j < last)
                def _():
                    if c == 0:
                        @pl.when(early | (back > 0))
                        def _():
                            remote(weo_v.at[0], we_v.at[j], we_s.at[0], we_r.at[j], owner(0)).wait_recv()

                    here = u_v.at[c, j]
                    here[0], here[1] = stepped(u_v.at[c, j + 1], we_v.at[j], x_v.at[c, 1 + j])

                @pl.when(base + j == last)
                def _():
                    u_v[c, j] = x_v[c, 1 + j]

                @pl.when((j == 0) & (base > 0) & jnp.logical_not(final_group))
                def _():
                    send_backward(c).start()

                @pl.when((j == 0) & final_group)
                def _():
                    left = u_v[c, 0].reshape(2 * width, no)
                    real, imag = combined(jnp.dot(left, we_v[SPAN - 1], preferred_element_type=F32))
                    x_v[c, 0, 0] = real.astype(BF16)
                    x_v[c, 0, 1] = imag.astype(BF16)
                    send_coupled(c).start()

                for l in range(2):
                    @pl.when((half_place == l) & is_home(j))
                    def _():
                        out_here(c, j, l).start()

                    @pl.when((half_place == l) & jnp.logical_not(is_home(j)))
                    def _():
                        out_far(c, j, l).start()

    for c in range(PARTS):
        for l in range(2):
            out_far(c, 0, l).wait_recv()
            handed(*a_args(c, l))

        @pl.when(core == 1)
        def _():
            @pl.loop(0, SPAN)
            def _(j):
                @pl.when(jnp.logical_not(is_home(j)))
                def _():
                    out_far(c, j, 0).wait_send()

            @pl.when(base < cuts - SPAN)
            def _():
                send_forward(c).wait_send()

            @pl.when(base > 0)
            def _():
                send_backward(c).wait_send()

        @pl.when(e < energies - 1)
        def _():
            halo_right(c).wait_send()

        @pl.when(e > 0)
        def _():
            halo_left(c).wait_send()

    @pl.when(shifts_out)
    def _():
        send_cm.wait_send()

    @pl.when(early)
    def _():
        for step in range(1, SPAN):
            share_cm(SPAN, step).wait_send()
        mate_cm(SPAN).wait_send()

    @pl.when(early)
    def _():
        for l in range(2):
            handed(*we_args(l))

    @pl.when(late)
    def _():
        for step in range(1, SPAN):
            ring_cm(step).wait_send()
        for l in range(2):
            handed(*it_args(l))
        for slot in range(SPAN):
            @pl.when(slot != place)
            def _():
                for step in range(1, SPAN):
                    share_cm(slot, step).wait_send()

                mate_cm(slot).wait_send()

        @pl.loop(0, SPAN - 1)
        def _(j):
            @pl.when(core == 1)
            def _():
                pass_on(j).wait_send()

            @pl.when(core == 0)
            def _():
                pass_back(j).wait_send()

def on_device(cuts, energies, inverse, coupling, pattern, source, previous, offsets, strength):
    no, nr = source.shape[4], source.shape[3]
    blocks = pattern.shape[-1]
    width = nr // PARTS
    dma = pltpu.SemaphoreType.DMA
    panel = pltpu.VMEM((2, 2, nr, no), BF16)
    stack = pltpu.VMEM((blocks, 2 * no // blocks, no), BF16)
    anywhere = pl.BlockSpec(memory_space=pl.ANY)
    scalars = pl.BlockSpec(memory_space=pltpu.SMEM)
    return pl.pallas_call(
        functools.partial(sweep_kernel, cuts, energies),
        name="sweeps",
        out_shape=jax.ShapeDtypeStruct(source.shape, BF16),
        in_specs=[anywhere, anywhere, scalars, anywhere, anywhere, scalars, scalars],
        out_specs=anywhere,
        scratch_shapes=[
            pltpu.VMEM((2, 2, no, no), BF16),
            pltpu.VMEM((2, no, 2 * no), BF16),
            pltpu.VMEM((2, no, no), BF16),
            stack, stack,
            pltpu.VMEM((SPAN + 1, blocks, 2 * no // blocks, no), BF16),
            pltpu.VMEM((2, no, 2 * no), BF16),
            pltpu.VMEM((2, no, 2 * no), BF16),
            pltpu.VMEM((SPAN, no, 2 * no), BF16),
            pltpu.VMEM((SPAN, no, 2 * no), BF16),
            pltpu.VMEM((SPAN, no, 2 * no), BF16),
            panel, panel, panel, panel,
            pltpu.VMEM((PARTS, 2, 2, width, no), BF16),
            pltpu.VMEM((PARTS, SPAN + 1, 2, width, no), BF16),
            pltpu.VMEM((PARTS, SPAN + 1, 2, width, no), BF16),
            dma((5,)),
            dma((PARTS,)), dma((PARTS,)), dma((PARTS,)), dma((PARTS,)),
            dma, dma,
            dma((SPAN - 1,)), dma((SPAN,)),
            dma(((SPAN - 1) * (SPAN + 1),)), dma(((SPAN - 1) * (SPAN + 1),)),
            dma((SPAN + 1,)), dma((SPAN + 1,)),
            dma((SPAN - 1,)), dma((SPAN - 1,)), dma((SPAN - 1,)),
            dma((2,)), dma((SPAN,)), dma((2,)), dma((SPAN,)),
            dma((2 * PARTS,)), dma((SPAN * PARTS,)),
            dma((PARTS,)), dma((PARTS,)), dma((PARTS,)), dma((PARTS,)),
            dma((SPAN * PARTS,)), dma((2 * PARTS,)),
        ],
        compiler_params=pltpu.CompilerParams(
            collective_id=0, has_side_effects=True, vmem_limit_bytes=60 << 20
        ),
    )(inverse, coupling, pattern, source, previous, offsets, strength)


def solution(mesh):
    return jax.shard_map(
        functools.partial(on_device, mesh.shape["cuts"], mesh.shape["energy"]),
        mesh=mesh,
        in_specs=(
            P(None, "energy", "cuts", None, None),
            P(None, "cuts", None, None),
            P("cuts", None, None),
            P(None, "energy", "cuts", None, None),
            P(None, "energy", "cuts", None, None),
            P(),
            P(),
        ),
        out_specs=P(None, "energy", "cuts", None, None),
        check_vma=False,
    )
```

```python
import functools

import jax
import jax.numpy as jnp
from jax import lax
from jax.experimental import pallas as pl
from jax.experimental.pallas import tpu as pltpu
from jax.sharding import PartitionSpec as P

MESH = pl.DeviceIdType.MESH
F32 = jnp.float32
BF16 = jnp.bfloat16
SPAN = 4
PARTS = 2


def combined(product):
    h, w = product.shape[0] // 2, product.shape[1] // 2
    real = product[:h, :w] - product[h:, w:]
    imag = product[:h, w:] + product[h:, :w]
    return real, imag


def sweep_kernel(
    cuts, energies, inv_ref, cpl_ref, pat_ref, src_ref, prev_ref, off_ref, str_ref, out_ref,
    inv_v, it_v, cpl_v, cm_v, cmt_v, cmr_v, wfo_v, weo_v, wf_v, we_v, itr_v, src_v, prev_v, hl_v, hr_v,
    ao_v, x_v, u_v,
    load_sem, hs_l, hs_r, hr_l, hr_r, cm_s, cm_r, ring_s, ring_r, cx_s, cx_r, cc_s, cc_r, fw_s, fw_r, fe_s, wf_s, wf_r, we_s, we_r, a_s, a_r,
    f_s, f_r, b_s, b_r, o_s, o_r,
):
    blocks = pat_ref.shape[-1]
    no = inv_v.shape[-1]
    nb = no // blocks
    width = src_v.shape[2] // PARTS
    pos = lax.axis_index("cuts")
    e = lax.axis_index("energy")
    core = lax.rem(e, 2)
    first_e = e - core
    last = cuts - 1
    place = lax.rem(pos, SPAN)
    base = pos - place
    stride = energies // SPAN
    x = lax.div(e, stride)
    late = base >= cuts // 2
    early = base < cuts // 2
    final_group = base == cuts - SPAN

    def rows(c):
        return pl.ds(c * width, width)

    def remote(src, dst, send, recv, device):
        return pltpu.make_async_remote_copy(
            src_ref=src, dst_ref=dst, send_sem=send, recv_sem=recv,
            device_id=device, device_id_type=MESH,
        )

    load_cpl = pltpu.make_async_copy(cpl_ref.at[:, 0], cpl_v, load_sem.at[0])
    load_inv = [
        pltpu.make_async_copy(inv_ref.at[:, l, 0], inv_v.at[l], load_sem.at[1 + l]) for l in range(2)
    ]
    load_src = pltpu.make_async_copy(src_ref.at[:, :, 0], src_v, load_sem.at[3])
    load_prev = pltpu.make_async_copy(prev_ref.at[:, :, 0], prev_v, load_sem.at[4])
    load_cpl.start()
    for copy in load_inv:
        copy.start()
    load_src.start()
    load_prev.start()

    def x_peer(step):
        return {"energy": lax.rem(x + step, SPAN) * stride + lax.rem(e, stride)}

    barrier = pltpu.get_barrier_semaphore()
    always = pos >= 0
    partners = [(always, {"energy": first_e + 1 - core})]
    for step in range(1, SPAN):
        there = base + lax.rem(place + step, SPAN)
        partners.append((always, {"cuts": there, "energy": first_e}))
        partners.append((always, {"cuts": there, "energy": first_e + 1}))
        partners.append((always, x_peer(step)))
    partners += [
        ((place == 0) & (pos > 0), {"cuts": pos - 1}),
        ((place == SPAN - 1) & (pos < last), {"cuts": pos + 1}),
        (pos >= SPAN, {"cuts": pos - SPAN}),
        (pos < cuts - SPAN, {"cuts": pos + SPAN}),
        ((core == 0) & (e > 0), {"energy": e - 1}),
        ((core == 1) & (e < energies - 1), {"energy": e + 1}),
    ]
    for there, device in partners:
        @pl.when(there)
        def _():
            pl.semaphore_signal(barrier, inc=1, device_id=device, device_id_type=MESH)

    def halo_right(c):
        return remote(prev_ref.at[:, :, 0, rows(c)], hl_v.at[:, :, rows(c)], hs_r.at[c], hr_l.at[c], {"energy": e + 1})

    def halo_left(c):
        return remote(prev_ref.at[:, :, 0, rows(c)], hr_v.at[:, :, rows(c)], hs_l.at[c], hr_r.at[c], {"energy": e - 1})

    load_cpl.wait()
    for a in range(blocks):
        for b in range(blocks):
            keep = pat_ref[0, a, b].astype(F32)
            lanes = slice(b * nb, (b + 1) * nb)
            real = cpl_v[0, a * nb:(a + 1) * nb, lanes].astype(F32)
            imag = cpl_v[1, a * nb:(a + 1) * nb, lanes].astype(F32)
            cm_v[a, :nb, lanes] = (real * (-keep)).astype(BF16)
            cm_v[a, nb:, lanes] = (imag * keep).astype(BF16)

    half = pl.ds(pl.multiple_of(core * nb, nb), nb)
    send_cm = remote(cm_v.at[x, half], cmr_v.at[SPAN, x, half], cm_s, cm_r, {"cuts": pos - 1})
    shifts_out = (pos > 0) & (pos <= cuts // 2)

    def in_ring(step):
        return {"cuts": base + lax.rem(place + step, SPAN)}

    def ring_cm(step):
        return remote(cm_v.at[x, half], cmr_v.at[place, x, half], ring_s.at[step - 1], ring_r.at[place], in_ring(step))

    def ringed_cm(slot):
        return remote(cm_v.at[x, half], cmr_v.at[slot, x, half], ring_s.at[0], ring_r.at[slot], in_ring(1))

    def share_cm(slot, step):
        piece = cmr_v.at[slot, x, half]
        n = (SPAN - 1) * slot + step - 1
        return remote(piece, piece, cx_s.at[n], cx_r.at[n], x_peer(step))

    def shared_cm(slot, step):
        piece = cmr_v.at[slot, lax.rem(x + SPAN - step, SPAN), half]
        n = (SPAN - 1) * slot + step - 1
        return remote(piece, piece, cx_s.at[n], cx_r.at[n], x_peer(step))

    def mate_cm(slot):
        piece = cmr_v.at[slot, :, half]
        return remote(piece, piece, cc_s.at[slot], cc_r.at[slot], {"energy": first_e + 1 - core})

    def pool_cm(slot):
        for step in range(1, SPAN):
            shared_cm(slot, step).wait_recv()

    for l in range(2):
        load_inv[l].wait()
        it_v[l, :, :no] = inv_v[l, 0].T
        it_v[l, :, no:] = inv_v[l, 1].T

    def product_into(left, right, target):
        product = jnp.dot(left[...].reshape(2 * no, no), right[...], preferred_element_type=F32)
        for t in range(blocks):
            real, imag = combined(product[2 * nb * t:2 * nb * (t + 1)])
            target[nb * t:nb * (t + 1), :no] = real.astype(BF16)
            target[nb * t:nb * (t + 1), no:] = imag.astype(BF16)

    def owner(l):
        return {"cuts": base + 2 * core + l, "energy": first_e + 1}

    def is_owner(l):
        return (core == 1) & (place == 2 + l)

    def is_far(l):
        return lax.rem(2 * core + l - place + SPAN, SPAN) == 2

    def hand(src, dst, l, send, recv):
        @pl.when(is_owner(l))
        def _():
            pltpu.make_async_copy(src, dst, recv).start()

        @pl.when(jnp.logical_not(is_owner(l)))
        def _():
            remote(src, dst, send, recv, owner(l)).start()

    def handed(src, dst, l, send, recv):
        @pl.when(jnp.logical_not(is_owner(l)))
        def _():
            remote(src, dst, send, recv, owner(l)).wait_send()

    def wf_args(l):
        return wfo_v.at[l], wf_v.at[place], l, wf_s.at[l], wf_r.at[place]

    def we_args(l):
        return weo_v.at[l], we_v.at[place], l, we_s.at[l], we_r.at[place]

    def it_args(l):
        return it_v.at[l], itr_v.at[place], l, wf_s.at[l], wf_r.at[place]

    def a_args(c, l):
        return ao_v.at[c, l], x_v.at[c, 1 + place], l, a_s.at[2 * c + l], a_r.at[PARTS * place + c]

    def turn(given):
        for t in range(blocks):
            lanes = slice(t * nb, (t + 1) * nb)
            real = given[t, :nb, :].T
            imag = -(given[t, nb:, :].T)
            for s in range(blocks):
                cmt_v[s, :nb, lanes] = real[s * nb:(s + 1) * nb]
                cmt_v[s, nb:, lanes] = imag[s * nb:(s + 1) * nb]

    @pl.when((pos > 0) & early)
    def _():
        turn(cm_v)

        @pl.loop(0, 2)
        def _(l):
            product_into(cmt_v, it_v.at[l], wfo_v.at[l])

    @pl.when(late)
    def _():
        cmr_v[place] = cm_v[...]

    pl.semaphore_wait(barrier, sum(jnp.where(there, 1, 0) for there, _ in partners))

    @pl.when(shifts_out)
    def _():
        send_cm.start()

    @pl.when(late)
    def _():
        for step in range(1, SPAN):
            ring_cm(step).start()

    for c in range(PARTS):
        @pl.when(e < energies - 1)
        def _():
            halo_right(c).start()

        @pl.when(e > 0)
        def _():
            halo_left(c).start()

    @pl.when((pos > 0) & early)
    def _():
        for l in range(2):
            hand(*wf_args(l))

    @pl.when(late)
    def _():
        for l in range(2):
            @pl.when(jnp.logical_not(is_far(l)))
            def _():
                hand(*it_args(l))

        for l in range(2):
            @pl.when(is_far(l))
            def _():
                hand(*it_args(l))

        for slot in range(SPAN):
            @pl.when(slot != place)
            def _():
                ringed_cm(slot).wait_recv()
                for step in range(1, SPAN):
                    share_cm(slot, step).start()
    @pl.when(early)
    def _():
        send_cm.wait_recv()
        for step in range(1, SPAN):
            share_cm(SPAN, step).start()

    @pl.when(early & (place < SPAN - 1))
    def _():
        pool_cm(SPAN)
        mate_cm(SPAN).start()

    near = F32(0)
    far = F32(0)
    for mode in range(off_ref.shape[0]):
        near = near + jnp.where(off_ref[mode] == 1, str_ref[mode], F32(0))
        far = far + jnp.where(off_ref[mode] == 2, str_ref[mode], F32(0))
    load_src.wait()
    load_prev.wait()

    @pl.when(e == 0)
    def _():
        hl_v[...] = jnp.zeros(hl_v.shape, BF16)

    @pl.when(e == energies - 1)
    def _():
        hr_v[...] = jnp.zeros(hr_v.shape, BF16)

    for c in range(PARTS):
        at = rows(c)

        @pl.when(e > 0)
        def _():
            halo_right(c).wait_recv()

        @pl.when(e < energies - 1)
        def _():
            halo_left(c).wait_recv()

        own = [prev_v[:, l, at, :].astype(F32) for l in range(2)]
        lo = [hl_v[:, l, at, :].astype(F32) for l in range(2)]
        hi = [hr_v[:, l, at, :].astype(F32) for l in range(2)]
        drives = (
            src_v[:, 0, at, :].astype(F32) + near * (own[1] + lo[1]) + far * (hi[0] + lo[0]),
            src_v[:, 1, at, :].astype(F32) + near * (hi[0] + own[0]) + far * (hi[1] + lo[1]),
        )
        for l in range(2):
            left = drives[l].astype(BF16).reshape(2 * width, no)
            real, imag = combined(jnp.dot(left, it_v[l], preferred_element_type=F32))
            ao_v[c, l, 0] = real.astype(BF16)
            ao_v[c, l, 1] = imag.astype(BF16)
            hand(*a_args(c, l))

    @pl.when(early & (place == SPAN - 1))
    def _():
        pool_cm(SPAN)
        mate_cm(SPAN).start()

    @pl.when(early)
    def _():
        mate_cm(SPAN).wait_recv()

        @pl.loop(0, 2)
        def _(l):
            product_into(cmr_v.at[SPAN], it_v.at[l], weo_v.at[l])

    @pl.when(early)
    def _():
        for l in range(2):
            hand(*we_args(l))

    @pl.when(late)
    def _():
        for slot in range(SPAN):
            @pl.when(slot != place)
            def _():
                pool_cm(slot)
                mate_cm(slot).start()

        for slot in range(SPAN):
            @pl.when(slot != place)
            def _():
                mate_cm(slot).wait_recv()

    def by_arrival(n):
        return lax.rem(place + jnp.where(n < 2, n, 5 - n), SPAN)

    def pass_on(j):
        return remote(itr_v.at[j], itr_v.at[j], fw_s.at[j], fw_r.at[j], {"energy": first_e + 1 - core})

    def pass_back(j):
        return remote(we_v.at[j], we_v.at[j], fe_s.at[j], we_r.at[j], {"energy": first_e + 1 - core})

    @pl.when(late & (core == 1))
    def _():
        @pl.loop(0, SPAN)
        def _(turn_no):
            j = by_arrival(turn_no)
            remote(it_v.at[0], itr_v.at[j], wf_s.at[0], wf_r.at[j], owner(0)).wait_recv()

            @pl.when(j < SPAN - 1)
            def _():
                pass_on(j).start()

            turn(cmr_v.at[j])
            product_into(cmt_v, itr_v.at[j], wf_v.at[j])

        @pl.when(final_group)
        def _():
            for t in range(blocks):
                we_v[SPAN - 1, nb * t:nb * (t + 1), :no] = cmr_v[0, t, :nb]
                we_v[SPAN - 1, nb * t:nb * (t + 1), no:] = cmr_v[0, t, nb:]

        @pl.when(jnp.logical_not(final_group))
        def _():
            we_v[SPAN - 1] = itr_v[SPAN - 1]

    @pl.when(late & (core == 0))
    def _():
        @pl.loop(0, SPAN)
        def _(turn_no):
            j = by_arrival(turn_no)

            @pl.when(j < SPAN - 1)
            def _():
                pass_on(j).wait_recv()
                product_into(cmr_v.at[j + 1], itr_v.at[j], we_v.at[j])
                pass_back(j).start()

    def stepped(given, weights, added):
        left = given[...].reshape(2 * width, no)
        real, imag = combined(jnp.dot(left, weights[...], preferred_element_type=F32))
        return (real + added[0].astype(F32)).astype(BF16), (imag + added[1].astype(F32)).astype(BF16)

    def send_forward(c):
        return remote(x_v.at[c, SPAN], x_v.at[c, 0], f_s.at[c], f_r.at[c], {"cuts": pos + SPAN})

    def send_backward(c):
        return remote(u_v.at[c, 0], u_v.at[c, SPAN], b_s.at[c], b_r.at[c], {"cuts": pos - SPAN})

    def send_coupled(c):
        return remote(x_v.at[c, 0], u_v.at[c, SPAN], b_s.at[c], b_r.at[c], {"cuts": pos - SPAN})

    def out_at(c, l):
        return out_ref.at[:, l, 0, rows(c)]

    def is_home(j):
        return (place >= 2) & (j == place)

    def out_far(c, j, l):
        device = {"cuts": base + j, "energy": first_e + lax.div(place, 2)}
        return remote(u_v.at[c, j], out_at(c, l), o_s.at[SPAN * c + j], o_r.at[2 * c + l], device)

    def out_here(c, j, l):
        return pltpu.make_async_copy(u_v.at[c, j], out_at(c, l), o_r.at[2 * c + l])

    half_place = lax.rem(place, 2)

    @pl.when(core == 1)
    def _():
        for c in range(PARTS):
            @pl.loop(0, SPAN)
            def _(j):
                remote(ao_v.at[c, 0], x_v.at[c, 1 + j], a_s.at[0], a_r.at[PARTS * j + c], owner(0)).wait_recv()

                @pl.when((j == 0) & (base > 0))
                def _():
                    send_forward(c).wait_recv()

                @pl.when(base + j > 0)
                def _():
                    if c == 0:
                        @pl.when(early)
                        def _():
                            remote(wfo_v.at[0], wf_v.at[j], wf_s.at[0], wf_r.at[j], owner(0)).wait_recv()

                    here = x_v.at[c, 1 + j]
                    here[0], here[1] = stepped(x_v.at[c, j], wf_v.at[j], here)

            @pl.when(base < cuts - SPAN)
            def _():
                send_forward(c).start()

        for c in range(PARTS):
            @pl.loop(0, SPAN)
            def _(back):
                j = SPAN - 1 - back

                @pl.when((back == 0) & (base < cuts - SPAN))
                def _():
                    send_backward(c).wait_recv()

                @pl.when(base + j < last)
                def _():
                    if c == 0:
                        @pl.when(early | (back > 0))
                        def _():
                            remote(weo_v.at[0], we_v.at[j], we_s.at[0], we_r.at[j], owner(0)).wait_recv()

                    here = u_v.at[c, j]
                    here[0], here[1] = stepped(u_v.at[c, j + 1], we_v.at[j], x_v.at[c, 1 + j])

                @pl.when(base + j == last)
                def _():
                    u_v[c, j] = x_v[c, 1 + j]

                @pl.when((j == 0) & (base > 0) & jnp.logical_not(final_group))
                def _():
                    send_backward(c).start()

                @pl.when((j == 0) & final_group)
                def _():
                    left = u_v[c, 0].reshape(2 * width, no)
                    real, imag = combined(jnp.dot(left, we_v[SPAN - 1], preferred_element_type=F32))
                    x_v[c, 0, 0] = real.astype(BF16)
                    x_v[c, 0, 1] = imag.astype(BF16)
                    send_coupled(c).start()

                for l in range(2):
                    @pl.when((half_place == l) & is_home(j))
                    def _():
                        out_here(c, j, l).start()

                    @pl.when((half_place == l) & jnp.logical_not(is_home(j)))
                    def _():
                        out_far(c, j, l).start()

    for c in range(PARTS):
        for l in range(2):
            out_far(c, 0, l).wait_recv()
            handed(*a_args(c, l))

        @pl.when(core == 1)
        def _():
            @pl.loop(0, SPAN)
            def _(j):
                @pl.when(jnp.logical_not(is_home(j)))
                def _():
                    out_far(c, j, 0).wait_send()

            @pl.when(base < cuts - SPAN)
            def _():
                send_forward(c).wait_send()

            @pl.when(base > 0)
            def _():
                send_backward(c).wait_send()

        @pl.when(e < energies - 1)
        def _():
            halo_right(c).wait_send()

        @pl.when(e > 0)
        def _():
            halo_left(c).wait_send()

    @pl.when(shifts_out)
    def _():
        send_cm.wait_send()

    @pl.when(early)
    def _():
        for step in range(1, SPAN):
            share_cm(SPAN, step).wait_send()
        mate_cm(SPAN).wait_send()

    @pl.when((pos > 0) & early)
    def _():
        for l in range(2):
            handed(*wf_args(l))

    @pl.when(early)
    def _():
        for l in range(2):
            handed(*we_args(l))

    @pl.when(late)
    def _():
        for step in range(1, SPAN):
            ring_cm(step).wait_send()
        for l in range(2):
            handed(*it_args(l))
        for slot in range(SPAN):
            @pl.when(slot != place)
            def _():
                for step in range(1, SPAN):
                    share_cm(slot, step).wait_send()

                mate_cm(slot).wait_send()

        @pl.loop(0, SPAN - 1)
        def _(j):
            @pl.when(core == 1)
            def _():
                pass_on(j).wait_send()

            @pl.when(core == 0)
            def _():
                pass_back(j).wait_send()

def on_device(cuts, energies, inverse, coupling, pattern, source, previous, offsets, strength):
    no, nr = source.shape[4], source.shape[3]
    blocks = pattern.shape[-1]
    width = nr // PARTS
    dma = pltpu.SemaphoreType.DMA
    panel = pltpu.VMEM((2, 2, nr, no), BF16)
    stack = pltpu.VMEM((blocks, 2 * no // blocks, no), BF16)
    anywhere = pl.BlockSpec(memory_space=pl.ANY)
    scalars = pl.BlockSpec(memory_space=pltpu.SMEM)
    return pl.pallas_call(
        functools.partial(sweep_kernel, cuts, energies),
        name="sweeps",
        out_shape=jax.ShapeDtypeStruct(source.shape, BF16),
        in_specs=[anywhere, anywhere, scalars, anywhere, anywhere, scalars, scalars],
        out_specs=anywhere,
        scratch_shapes=[
            pltpu.VMEM((2, 2, no, no), BF16),
            pltpu.VMEM((2, no, 2 * no), BF16),
            pltpu.VMEM((2, no, no), BF16),
            stack, stack,
            pltpu.VMEM((SPAN + 1, blocks, 2 * no // blocks, no), BF16),
            pltpu.VMEM((2, no, 2 * no), BF16),
            pltpu.VMEM((2, no, 2 * no), BF16),
            pltpu.VMEM((SPAN, no, 2 * no), BF16),
            pltpu.VMEM((SPAN, no, 2 * no), BF16),
            pltpu.VMEM((SPAN, no, 2 * no), BF16),
            panel, panel, panel, panel,
            pltpu.VMEM((PARTS, 2, 2, width, no), BF16),
            pltpu.VMEM((PARTS, SPAN + 1, 2, width, no), BF16),
            pltpu.VMEM((PARTS, SPAN + 1, 2, width, no), BF16),
            dma((5,)),
            dma((PARTS,)), dma((PARTS,)), dma((PARTS,)), dma((PARTS,)),
            dma, dma,
            dma((SPAN - 1,)), dma((SPAN,)),
            dma(((SPAN - 1) * (SPAN + 1),)), dma(((SPAN - 1) * (SPAN + 1),)),
            dma((SPAN + 1,)), dma((SPAN + 1,)),
            dma((SPAN - 1,)), dma((SPAN - 1,)), dma((SPAN - 1,)),
            dma((2,)), dma((SPAN,)), dma((2,)), dma((SPAN,)),
            dma((2 * PARTS,)), dma((SPAN * PARTS,)),
            dma((PARTS,)), dma((PARTS,)), dma((PARTS,)), dma((PARTS,)),
            dma((SPAN * PARTS,)), dma((2 * PARTS,)),
        ],
        compiler_params=pltpu.CompilerParams(
            collective_id=0, has_side_effects=True, vmem_limit_bytes=60 << 20
        ),
    )(inverse, coupling, pattern, source, previous, offsets, strength)


def solution(mesh):
    return jax.shard_map(
        functools.partial(on_device, mesh.shape["cuts"], mesh.shape["energy"]),
        mesh=mesh,
        in_specs=(
            P(None, "energy", "cuts", None, None),
            P(None, "cuts", None, None),
            P("cuts", None, None),
            P(None, "energy", "cuts", None, None),
            P(None, "energy", "cuts", None, None),
            P(),
            P(),
        ),
        out_specs=P(None, "energy", "cuts", None, None),
        check_vma=False,
    )
```

```python
import functools

import jax
import jax.numpy as jnp
from jax import lax
from jax.experimental import pallas as pl
from jax.experimental.pallas import tpu as pltpu
from jax.sharding import PartitionSpec as P

MESH = pl.DeviceIdType.MESH
F32 = jnp.float32
BF16 = jnp.bfloat16
SPAN = 4
PARTS = 2


def combined(product):
    h, w = product.shape[0] // 2, product.shape[1] // 2
    real = product[:h, :w] - product[h:, w:]
    imag = product[:h, w:] + product[h:, :w]
    return real, imag


def sweep_kernel(
    cuts, energies, inv_ref, cpl_ref, pat_ref, src_ref, prev_ref, off_ref, str_ref, out_ref,
    inv_v, it_v, cpl_v, cm_v, cmt_v, cmr_v, wfo_v, weo_v, wf_v, we_v, itr_v, src_v, prev_v, hl_v, hr_v,
    ao_v, x_v, u_v,
    load_sem, hs_l, hs_r, hr_l, hr_r, cm_s, cm_r, ring_s, ring_r, cx_s, cx_r, cc_s, cc_r, fw_s, fw_r, fe_s, wf_s, wf_r, we_s, we_r, a_s, a_r,
    f_s, f_r, b_s, b_r, o_s, o_r,
):
    blocks = pat_ref.shape[-1]
    no = inv_v.shape[-1]
    nb = no // blocks
    width = src_v.shape[2] // PARTS
    pos = lax.axis_index("cuts")
    e = lax.axis_index("energy")
    core = lax.rem(e, 2)
    first_e = e - core
    last = cuts - 1
    place = lax.rem(pos, SPAN)
    base = pos - place
    stride = energies // SPAN
    x = lax.div(e, stride)
    late = base >= cuts // 2
    early = base < cuts // 2
    final_group = base == cuts - SPAN

    def rows(c):
        return pl.ds(c * width, width)

    def remote(src, dst, send, recv, device):
        return pltpu.make_async_remote_copy(
            src_ref=src, dst_ref=dst, send_sem=send, recv_sem=recv,
            device_id=device, device_id_type=MESH,
        )

    load_cpl = pltpu.make_async_copy(cpl_ref.at[:, 0], cpl_v, load_sem.at[0])
    load_inv = [
        pltpu.make_async_copy(inv_ref.at[:, l, 0], inv_v.at[l], load_sem.at[1 + l]) for l in range(2)
    ]
    load_src = pltpu.make_async_copy(src_ref.at[:, :, 0], src_v, load_sem.at[3])
    load_prev = pltpu.make_async_copy(prev_ref.at[:, :, 0], prev_v, load_sem.at[4])
    load_cpl.start()
    for copy in load_inv:
        copy.start()
    load_src.start()
    load_prev.start()

    def x_peer(step):
        return {"energy": lax.rem(x + step, SPAN) * stride + lax.rem(e, stride)}

    barrier = pltpu.get_barrier_semaphore()
    always = pos >= 0
    partners = [(always, {"energy": first_e + 1 - core})]
    for step in range(1, SPAN):
        there = base + lax.rem(place + step, SPAN)
        partners.append((always, {"cuts": there, "energy": first_e}))
        partners.append((always, {"cuts": there, "energy": first_e + 1}))
        partners.append((always, x_peer(step)))
    partners += [
        ((place == 0) & (pos > 0), {"cuts": pos - 1}),
        ((place == SPAN - 1) & (pos < last), {"cuts": pos + 1}),
        (pos >= SPAN, {"cuts": pos - SPAN}),
        (pos < cuts - SPAN, {"cuts": pos + SPAN}),
        ((core == 0) & (e > 0), {"energy": e - 1}),
        ((core == 1) & (e < energies - 1), {"energy": e + 1}),
    ]
    for there, device in partners:
        @pl.when(there)
        def _():
            pl.semaphore_signal(barrier, inc=1, device_id=device, device_id_type=MESH)

    def halo_right(c):
        return remote(prev_ref.at[:, :, 0, rows(c)], hl_v.at[:, :, rows(c)], hs_r.at[c], hr_l.at[c], {"energy": e + 1})

    def halo_left(c):
        return remote(prev_ref.at[:, :, 0, rows(c)], hr_v.at[:, :, rows(c)], hs_l.at[c], hr_r.at[c], {"energy": e - 1})

    load_cpl.wait()
    for a in range(blocks):
        for b in range(blocks):
            keep = pat_ref[0, a, b].astype(F32)
            lanes = slice(b * nb, (b + 1) * nb)
            real = cpl_v[0, a * nb:(a + 1) * nb, lanes].astype(F32)
            imag = cpl_v[1, a * nb:(a + 1) * nb, lanes].astype(F32)
            cm_v[a, :nb, lanes] = (real * (-keep)).astype(BF16)
            cm_v[a, nb:, lanes] = (imag * keep).astype(BF16)

    half = pl.ds(pl.multiple_of(core * nb, nb), nb)
    send_cm = remote(cm_v.at[x, half], cmr_v.at[SPAN, x, half], cm_s, cm_r, {"cuts": pos - 1})
    shifts_out = (pos > 0) & (pos <= cuts // 2)

    def in_ring(step):
        return {"cuts": base + lax.rem(place + step, SPAN)}

    def ring_cm(step):
        return remote(cm_v.at[x, half], cmr_v.at[place, x, half], ring_s.at[step - 1], ring_r.at[place], in_ring(step))

    def ringed_cm(slot):
        return remote(cm_v.at[x, half], cmr_v.at[slot, x, half], ring_s.at[0], ring_r.at[slot], in_ring(1))

    def share_cm(slot, step):
        piece = cmr_v.at[slot, x, half]
        n = (SPAN - 1) * slot + step - 1
        return remote(piece, piece, cx_s.at[n], cx_r.at[n], x_peer(step))

    def shared_cm(slot, step):
        piece = cmr_v.at[slot, lax.rem(x + SPAN - step, SPAN), half]
        n = (SPAN - 1) * slot + step - 1
        return remote(piece, piece, cx_s.at[n], cx_r.at[n], x_peer(step))

    def mate_cm(slot):
        piece = cmr_v.at[slot, :, half]
        return remote(piece, piece, cc_s.at[slot], cc_r.at[slot], {"energy": first_e + 1 - core})

    def pool_cm(slot):
        for step in range(1, SPAN):
            shared_cm(slot, step).wait_recv()

    def load_it(l):
        load_inv[l].wait()
        it_v[l, :, :no] = inv_v[l, 0].T
        it_v[l, :, no:] = inv_v[l, 1].T

    def is_far(l):
        return lax.rem(2 * core + l - place + SPAN, SPAN) == 2

    lead = jnp.where(is_far(1), 1, 0)

    @pl.when(lead == 0)
    def _():
        load_it(0)

    @pl.when(lead == 1)
    def _():
        load_it(1)

    def product_into(left, right, target):
        product = jnp.dot(left[...].reshape(2 * no, no), right[...], preferred_element_type=F32)
        for t in range(blocks):
            real, imag = combined(product[2 * nb * t:2 * nb * (t + 1)])
            target[nb * t:nb * (t + 1), :no] = real.astype(BF16)
            target[nb * t:nb * (t + 1), no:] = imag.astype(BF16)

    def owner(l):
        return {"cuts": base + 2 * core + l, "energy": first_e + 1}

    def is_owner(l):
        return (core == 1) & (place == 2 + l)

    def hand(src, dst, l, send, recv):
        @pl.when(is_owner(l))
        def _():
            pltpu.make_async_copy(src, dst, recv).start()

        @pl.when(jnp.logical_not(is_owner(l)))
        def _():
            remote(src, dst, send, recv, owner(l)).start()

    def handed(src, dst, l, send, recv):
        @pl.when(jnp.logical_not(is_owner(l)))
        def _():
            remote(src, dst, send, recv, owner(l)).wait_send()

    def wf_args(l):
        return wfo_v.at[l], wf_v.at[place], l, wf_s.at[l], wf_r.at[place]

    def we_args(l):
        return weo_v.at[l], we_v.at[place], l, we_s.at[l], we_r.at[place]

    def it_args(l):
        return it_v.at[l], itr_v.at[place], l, wf_s.at[l], wf_r.at[place]

    def a_args(c, l):
        return ao_v.at[c, l], x_v.at[c, 1 + place], l, a_s.at[2 * c + l], a_r.at[PARTS * place + c]

    def turn(given):
        for t in range(blocks):
            lanes = slice(t * nb, (t + 1) * nb)
            real = given[t, :nb, :].T
            imag = -(given[t, nb:, :].T)
            for s in range(blocks):
                cmt_v[s, :nb, lanes] = real[s * nb:(s + 1) * nb]
                cmt_v[s, nb:, lanes] = imag[s * nb:(s + 1) * nb]

    @pl.when((pos > 0) & early)
    def _():
        turn(cm_v)
        product_into(cmt_v, it_v.at[lead], wfo_v.at[lead])

    @pl.when(late | (pos == 0))
    def _():
        for l in range(2):
            @pl.when(lead != l)
            def _():
                load_it(l)

    @pl.when(late)
    def _():
        cmr_v[place] = cm_v[...]

    pl.semaphore_wait(barrier, sum(jnp.where(there, 1, 0) for there, _ in partners))

    @pl.when(shifts_out)
    def _():
        send_cm.start()

    @pl.when(late)
    def _():
        for step in range(1, SPAN):
            ring_cm(step).start()

    def start_halos():
        for c in range(PARTS):
            @pl.when(e < energies - 1)
            def _():
                halo_right(c).start()

            @pl.when(e > 0)
            def _():
                halo_left(c).start()

    @pl.when(base == 0)
    def _():
        start_halos()

    @pl.when((pos > 0) & early)
    def _():
        for l in range(2):
            @pl.when(lead == l)
            def _():
                hand(*wf_args(l))
                load_it(1 - l)

        product_into(cmt_v, it_v.at[1 - lead], wfo_v.at[1 - lead])
        for l in range(2):
            @pl.when(lead != l)
            def _():
                hand(*wf_args(l))

    @pl.when(late)
    def _():
        for l in range(2):
            @pl.when(jnp.logical_not(is_far(l)))
            def _():
                hand(*it_args(l))

        for l in range(2):
            @pl.when(is_far(l))
            def _():
                hand(*it_args(l))

        start_halos()
        for slot in range(SPAN):
            @pl.when(slot != place)
            def _():
                ringed_cm(slot).wait_recv()
                for step in range(1, SPAN):
                    share_cm(slot, step).start()
    @pl.when(base == SPAN)
    def _():
        start_halos()

    @pl.when(early)
    def _():
        send_cm.wait_recv()
        for step in range(1, SPAN):
            share_cm(SPAN, step).start()

    @pl.when(early & (place < SPAN - 1))
    def _():
        pool_cm(SPAN)
        mate_cm(SPAN).start()

    near = F32(0)
    far = F32(0)
    for mode in range(off_ref.shape[0]):
        near = near + jnp.where(off_ref[mode] == 1, str_ref[mode], F32(0))
        far = far + jnp.where(off_ref[mode] == 2, str_ref[mode], F32(0))
    load_src.wait()
    load_prev.wait()

    @pl.when(e == 0)
    def _():
        hl_v[...] = jnp.zeros(hl_v.shape, BF16)

    @pl.when(e == energies - 1)
    def _():
        hr_v[...] = jnp.zeros(hr_v.shape, BF16)

    for c in range(PARTS):
        at = rows(c)

        @pl.when(e > 0)
        def _():
            halo_right(c).wait_recv()

        @pl.when(e < energies - 1)
        def _():
            halo_left(c).wait_recv()

        own = [prev_v[:, l, at, :].astype(F32) for l in range(2)]
        lo = [hl_v[:, l, at, :].astype(F32) for l in range(2)]
        hi = [hr_v[:, l, at, :].astype(F32) for l in range(2)]
        drives = (
            src_v[:, 0, at, :].astype(F32) + near * (own[1] + lo[1]) + far * (hi[0] + lo[0]),
            src_v[:, 1, at, :].astype(F32) + near * (hi[0] + own[0]) + far * (hi[1] + lo[1]),
        )
        for l in range(2):
            left = drives[l].astype(BF16).reshape(2 * width, no)
            real, imag = combined(jnp.dot(left, it_v[l], preferred_element_type=F32))
            ao_v[c, l, 0] = real.astype(BF16)
            ao_v[c, l, 1] = imag.astype(BF16)
            hand(*a_args(c, l))

    @pl.when(early & (place == SPAN - 1))
    def _():
        pool_cm(SPAN)
        mate_cm(SPAN).start()

    @pl.when(early)
    def _():
        mate_cm(SPAN).wait_recv()

        @pl.loop(0, 2)
        def _(n):
            l = jnp.where(n == 0, lead, 1 - lead)
            product_into(cmr_v.at[SPAN], it_v.at[l], weo_v.at[l])
            hand(*we_args(l))

    @pl.when(late)
    def _():
        for slot in range(SPAN):
            @pl.when(slot != place)
            def _():
                pool_cm(slot)
                mate_cm(slot).start()

        for slot in range(SPAN):
            @pl.when(slot != place)
            def _():
                mate_cm(slot).wait_recv()

    def by_arrival(n):
        return lax.rem(place + jnp.where(n < 2, n, 5 - n), SPAN)

    def pass_on(j):
        return remote(itr_v.at[j], itr_v.at[j], fw_s.at[j], fw_r.at[j], {"energy": first_e + 1 - core})

    def pass_back(j):
        return remote(we_v.at[j], we_v.at[j], fe_s.at[j], we_r.at[j], {"energy": first_e + 1 - core})

    @pl.when(late & (core == 1))
    def _():
        @pl.loop(0, SPAN)
        def _(turn_no):
            j = by_arrival(turn_no)
            remote(it_v.at[0], itr_v.at[j], wf_s.at[0], wf_r.at[j], owner(0)).wait_recv()

            @pl.when(j < SPAN - 1)
            def _():
                pass_on(j).start()

            turn(cmr_v.at[j])
            product_into(cmt_v, itr_v.at[j], wf_v.at[j])

        @pl.when(final_group)
        def _():
            for t in range(blocks):
                we_v[SPAN - 1, nb * t:nb * (t + 1), :no] = cmr_v[0, t, :nb]
                we_v[SPAN - 1, nb * t:nb * (t + 1), no:] = cmr_v[0, t, nb:]

        @pl.when(jnp.logical_not(final_group))
        def _():
            we_v[SPAN - 1] = itr_v[SPAN - 1]

    @pl.when(late & (core == 0))
    def _():
        @pl.loop(0, SPAN)
        def _(turn_no):
            j = by_arrival(turn_no)

            @pl.when(j < SPAN - 1)
            def _():
                pass_on(j).wait_recv()
                product_into(cmr_v.at[j + 1], itr_v.at[j], we_v.at[j])
                pass_back(j).start()

    def stepped(given, weights, added):
        left = given[...].reshape(2 * width, no)
        real, imag = combined(jnp.dot(left, weights[...], preferred_element_type=F32))
        return (real + added[0].astype(F32)).astype(BF16), (imag + added[1].astype(F32)).astype(BF16)

    def send_forward(c):
        return remote(x_v.at[c, SPAN], x_v.at[c, 0], f_s.at[c], f_r.at[c], {"cuts": pos + SPAN})

    def send_backward(c):
        return remote(u_v.at[c, 0], u_v.at[c, SPAN], b_s.at[c], b_r.at[c], {"cuts": pos - SPAN})

    def send_coupled(c):
        return remote(x_v.at[c, 0], u_v.at[c, SPAN], b_s.at[c], b_r.at[c], {"cuts": pos - SPAN})

    def out_at(c, l):
        return out_ref.at[:, l, 0, rows(c)]

    def is_home(j):
        return (place >= 2) & (j == place)

    def out_far(c, j, l):
        device = {"cuts": base + j, "energy": first_e + lax.div(place, 2)}
        return remote(u_v.at[c, j], out_at(c, l), o_s.at[SPAN * c + j], o_r.at[2 * c + l], device)

    def out_here(c, j, l):
        return pltpu.make_async_copy(u_v.at[c, j], out_at(c, l), o_r.at[2 * c + l])

    half_place = lax.rem(place, 2)

    @pl.when(core == 1)
    def _():
        for c in range(PARTS):
            for j in range(SPAN):
                remote(ao_v.at[c, 0], x_v.at[c, 1 + j], a_s.at[0], a_r.at[PARTS * j + c], owner(0)).wait_recv()

                @pl.when((j == 0) & (base > 0))
                def _():
                    send_forward(c).wait_recv()

                @pl.when(base + j > 0)
                def _(j=j):
                    if c == 0:
                        @pl.when(early)
                        def _():
                            remote(wfo_v.at[0], wf_v.at[j], wf_s.at[0], wf_r.at[j], owner(0)).wait_recv()

                    here = x_v.at[c, 1 + j]
                    here[0], here[1] = stepped(x_v.at[c, j], wf_v.at[j], here)

            @pl.when(base < cuts - SPAN)
            def _():
                send_forward(c).start()

        for c in range(PARTS):
            for back in range(SPAN):
                j = SPAN - 1 - back

                @pl.when((back == 0) & (base < cuts - SPAN))
                def _():
                    send_backward(c).wait_recv()

                @pl.when(base + j < last)
                def _():
                    if c == 0:
                        @pl.when(early | (back > 0))
                        def _():
                            remote(weo_v.at[0], we_v.at[j], we_s.at[0], we_r.at[j], owner(0)).wait_recv()

                    here = u_v.at[c, j]
                    here[0], here[1] = stepped(u_v.at[c, j + 1], we_v.at[j], x_v.at[c, 1 + j])

                @pl.when(base + j == last)
                def _():
                    u_v[c, j] = x_v[c, 1 + j]

                @pl.when((j == 0) & (base > 0) & jnp.logical_not(final_group))
                def _():
                    send_backward(c).start()

                @pl.when((j == 0) & final_group)
                def _():
                    left = u_v[c, 0].reshape(2 * width, no)
                    real, imag = combined(jnp.dot(left, we_v[SPAN - 1], preferred_element_type=F32))
                    x_v[c, 0, 0] = real.astype(BF16)
                    x_v[c, 0, 1] = imag.astype(BF16)
                    send_coupled(c).start()

                for l in range(2):
                    @pl.when((half_place == l) & is_home(j))
                    def _():
                        out_here(c, j, l).start()

                    @pl.when((half_place == l) & jnp.logical_not(is_home(j)))
                    def _():
                        out_far(c, j, l).start()

    for c in range(PARTS):
        for l in range(2):
            out_far(c, 0, l).wait_recv()
            handed(*a_args(c, l))

        @pl.when(core == 1)
        def _():
            @pl.loop(0, SPAN)
            def _(j):
                @pl.when(jnp.logical_not(is_home(j)))
                def _():
                    out_far(c, j, 0).wait_send()

            @pl.when(base < cuts - SPAN)
            def _():
                send_forward(c).wait_send()

            @pl.when(base > 0)
            def _():
                send_backward(c).wait_send()

        @pl.when(e < energies - 1)
        def _():
            halo_right(c).wait_send()

        @pl.when(e > 0)
        def _():
            halo_left(c).wait_send()

    @pl.when(shifts_out)
    def _():
        send_cm.wait_send()

    @pl.when(early)
    def _():
        for step in range(1, SPAN):
            share_cm(SPAN, step).wait_send()
        mate_cm(SPAN).wait_send()

    @pl.when((pos > 0) & early)
    def _():
        for l in range(2):
            handed(*wf_args(l))

    @pl.when(early)
    def _():
        for l in range(2):
            handed(*we_args(l))

    @pl.when(late)
    def _():
        for step in range(1, SPAN):
            ring_cm(step).wait_send()
        for l in range(2):
            handed(*it_args(l))
        for slot in range(SPAN):
            @pl.when(slot != place)
            def _():
                for step in range(1, SPAN):
                    share_cm(slot, step).wait_send()

                mate_cm(slot).wait_send()

        @pl.loop(0, SPAN - 1)
        def _(j):
            @pl.when(core == 1)
            def _():
                pass_on(j).wait_send()

            @pl.when(core == 0)
            def _():
                pass_back(j).wait_send()

def on_device(cuts, energies, inverse, coupling, pattern, source, previous, offsets, strength):
    no, nr = source.shape[4], source.shape[3]
    blocks = pattern.shape[-1]
    width = nr // PARTS
    dma = pltpu.SemaphoreType.DMA
    panel = pltpu.VMEM((2, 2, nr, no), BF16)
    stack = pltpu.VMEM((blocks, 2 * no // blocks, no), BF16)
    anywhere = pl.BlockSpec(memory_space=pl.ANY)
    scalars = pl.BlockSpec(memory_space=pltpu.SMEM)
    return pl.pallas_call(
        functools.partial(sweep_kernel, cuts, energies),
        name="sweeps",
        out_shape=jax.ShapeDtypeStruct(source.shape, BF16),
        in_specs=[anywhere, anywhere, scalars, anywhere, anywhere, scalars, scalars],
        out_specs=anywhere,
        scratch_shapes=[
            pltpu.VMEM((2, 2, no, no), BF16),
            pltpu.VMEM((2, no, 2 * no), BF16),
            pltpu.VMEM((2, no, no), BF16),
            stack, stack,
            pltpu.VMEM((SPAN + 1, blocks, 2 * no // blocks, no), BF16),
            pltpu.VMEM((2, no, 2 * no), BF16),
            pltpu.VMEM((2, no, 2 * no), BF16),
            pltpu.VMEM((SPAN, no, 2 * no), BF16),
            pltpu.VMEM((SPAN, no, 2 * no), BF16),
            pltpu.VMEM((SPAN, no, 2 * no), BF16),
            panel, panel, panel, panel,
            pltpu.VMEM((PARTS, 2, 2, width, no), BF16),
            pltpu.VMEM((PARTS, SPAN + 1, 2, width, no), BF16),
            pltpu.VMEM((PARTS, SPAN + 1, 2, width, no), BF16),
            dma((5,)),
            dma((PARTS,)), dma((PARTS,)), dma((PARTS,)), dma((PARTS,)),
            dma, dma,
            dma((SPAN - 1,)), dma((SPAN,)),
            dma(((SPAN - 1) * (SPAN + 1),)), dma(((SPAN - 1) * (SPAN + 1),)),
            dma((SPAN + 1,)), dma((SPAN + 1,)),
            dma((SPAN - 1,)), dma((SPAN - 1,)), dma((SPAN - 1,)),
            dma((2,)), dma((SPAN,)), dma((2,)), dma((SPAN,)),
            dma((2 * PARTS,)), dma((SPAN * PARTS,)),
            dma((PARTS,)), dma((PARTS,)), dma((PARTS,)), dma((PARTS,)),
            dma((SPAN * PARTS,)), dma((2 * PARTS,)),
        ],
        compiler_params=pltpu.CompilerParams(
            collective_id=0, has_side_effects=True, vmem_limit_bytes=60 << 20
        ),
    )(inverse, coupling, pattern, source, previous, offsets, strength)


def solution(mesh):
    return jax.shard_map(
        functools.partial(on_device, mesh.shape["cuts"], mesh.shape["energy"]),
        mesh=mesh,
        in_specs=(
            P(None, "energy", "cuts", None, None),
            P(None, "cuts", None, None),
            P("cuts", None, None),
            P(None, "energy", "cuts", None, None),
            P(None, "energy", "cuts", None, None),
            P(),
            P(),
        ),
        out_specs=P(None, "energy", "cuts", None, None),
        check_vma=False,
    )
```

```python
import functools

import jax
import jax.numpy as jnp
from jax import lax
from jax.experimental import pallas as pl
from jax.experimental.pallas import tpu as pltpu
from jax.sharding import PartitionSpec as P

MESH = pl.DeviceIdType.MESH
F32 = jnp.float32
BF16 = jnp.bfloat16
SPAN = 4
PARTS = 2


def combined(product):
    h, w = product.shape[0] // 2, product.shape[1] // 2
    real = product[:h, :w] - product[h:, w:]
    imag = product[:h, w:] + product[h:, :w]
    return real, imag


def sweep_kernel(
    cuts, energies, inv_ref, cpl_ref, pat_ref, src_ref, prev_ref, off_ref, str_ref, out_ref,
    inv_v, it_v, cpl_v, cm_v, cmt_v, cmr_v, wfo_v, weo_v, wf_v, we_v, itr_v, src_v, prev_v, hl_v, hr_v,
    ao_v, x_v, u_v,
    load_sem, hs_l, hs_r, hr_l, hr_r, cm_s, cm_r, ring_s, ring_r, cx_s, cx_r, cc_s, cc_r, fw_s, fw_r, fe_s, wf_s, wf_r, we_s, we_r, a_s, a_r,
    f_s, f_r, b_s, b_r, o_s, o_r,
):
    blocks = pat_ref.shape[-1]
    no = inv_v.shape[-1]
    nb = no // blocks
    width = src_v.shape[2] // PARTS
    pos = lax.axis_index("cuts")
    e = lax.axis_index("energy")
    core = lax.rem(e, 2)
    first_e = e - core
    last = cuts - 1
    place = lax.rem(pos, SPAN)
    base = pos - place
    stride = energies // SPAN
    x = lax.div(e, stride)
    late = base >= cuts // 2
    early = base < cuts // 2
    final_group = base == cuts - SPAN

    def rows(c):
        return pl.ds(c * width, width)

    def remote(src, dst, send, recv, device):
        return pltpu.make_async_remote_copy(
            src_ref=src, dst_ref=dst, send_sem=send, recv_sem=recv,
            device_id=device, device_id_type=MESH,
        )

    load_cpl = pltpu.make_async_copy(cpl_ref.at[:, 0], cpl_v, load_sem.at[0])
    load_inv = [
        pltpu.make_async_copy(inv_ref.at[:, l, 0], inv_v.at[l], load_sem.at[1 + l]) for l in range(2)
    ]
    load_src = pltpu.make_async_copy(src_ref.at[:, :, 0], src_v, load_sem.at[3])
    load_prev = pltpu.make_async_copy(prev_ref.at[:, :, 0], prev_v, load_sem.at[4])
    load_cpl.start()

    def is_far(l):
        return lax.rem(2 * core + l - place + SPAN, SPAN) == 2

    lead = jnp.where(is_far(1), 1, 0)
    for l in range(2):
        @pl.when(lead == l)
        def _():
            load_inv[l].start()
            load_inv[1 - l].start()

    def x_peer(step):
        return {"energy": lax.rem(x + step, SPAN) * stride + lax.rem(e, stride)}

    barrier = pltpu.get_barrier_semaphore()
    always = pos >= 0
    partners = [(always, {"energy": first_e + 1 - core})]
    for step in range(1, SPAN):
        there = base + lax.rem(place + step, SPAN)
        partners.append((always, {"cuts": there, "energy": first_e}))
        partners.append((always, {"cuts": there, "energy": first_e + 1}))
        partners.append((always, x_peer(step)))
    partners += [
        ((place == 0) & (pos > 0), {"cuts": pos - 1}),
        ((place == SPAN - 1) & (pos < last), {"cuts": pos + 1}),
        (pos >= SPAN, {"cuts": pos - SPAN}),
        (pos < cuts - SPAN, {"cuts": pos + SPAN}),
        ((core == 0) & (e > 0), {"energy": e - 1}),
        ((core == 1) & (e < energies - 1), {"energy": e + 1}),
    ]
    for there, device in partners:
        @pl.when(there)
        def _():
            pl.semaphore_signal(barrier, inc=1, device_id=device, device_id_type=MESH)

    def halo_right(c):
        return remote(prev_ref.at[:, :, 0, rows(c)], hl_v.at[:, :, rows(c)], hs_r.at[c], hr_l.at[c], {"energy": e + 1})

    def halo_left(c):
        return remote(prev_ref.at[:, :, 0, rows(c)], hr_v.at[:, :, rows(c)], hs_l.at[c], hr_r.at[c], {"energy": e - 1})

    load_cpl.wait()
    for a in range(blocks):
        for b in range(blocks):
            keep = pat_ref[0, a, b].astype(F32)
            lanes = slice(b * nb, (b + 1) * nb)
            real = cpl_v[0, a * nb:(a + 1) * nb, lanes].astype(F32)
            imag = cpl_v[1, a * nb:(a + 1) * nb, lanes].astype(F32)
            cm_v[a, :nb, lanes] = (real * (-keep)).astype(BF16)
            cm_v[a, nb:, lanes] = (imag * keep).astype(BF16)

    half = pl.ds(pl.multiple_of(core * nb, nb), nb)
    send_cm = remote(cm_v.at[x, half], cmr_v.at[SPAN, x, half], cm_s, cm_r, {"cuts": pos - 1})
    shifts_out = (pos > 0) & (pos <= cuts // 2)

    def in_ring(step):
        return {"cuts": base + lax.rem(place + step, SPAN)}

    def ring_cm(step):
        return remote(cm_v.at[x, half], cmr_v.at[place, x, half], ring_s.at[step - 1], ring_r.at[place], in_ring(step))

    def ringed_cm(slot):
        return remote(cm_v.at[x, half], cmr_v.at[slot, x, half], ring_s.at[0], ring_r.at[slot], in_ring(1))

    def share_cm(slot, step):
        piece = cmr_v.at[slot, x, half]
        n = (SPAN - 1) * slot + step - 1
        return remote(piece, piece, cx_s.at[n], cx_r.at[n], x_peer(step))

    def shared_cm(slot, step):
        piece = cmr_v.at[slot, lax.rem(x + SPAN - step, SPAN), half]
        n = (SPAN - 1) * slot + step - 1
        return remote(piece, piece, cx_s.at[n], cx_r.at[n], x_peer(step))

    def mate_cm(slot):
        piece = cmr_v.at[slot, :, half]
        return remote(piece, piece, cc_s.at[slot], cc_r.at[slot], {"energy": first_e + 1 - core})

    def pool_cm(slot):
        for step in range(1, SPAN):
            shared_cm(slot, step).wait_recv()

    def load_it(l):
        load_inv[l].wait()
        it_v[l, :, :no] = inv_v[l, 0].T
        it_v[l, :, no:] = inv_v[l, 1].T

    @pl.when(lead == 0)
    def _():
        load_it(0)

    @pl.when(lead == 1)
    def _():
        load_it(1)

    def product_into(left, right, target):
        product = jnp.dot(left[...].reshape(2 * no, no), right[...], preferred_element_type=F32)
        for t in range(blocks):
            real, imag = combined(product[2 * nb * t:2 * nb * (t + 1)])
            target[nb * t:nb * (t + 1), :no] = real.astype(BF16)
            target[nb * t:nb * (t + 1), no:] = imag.astype(BF16)

    def owner(l):
        return {"cuts": base + 2 * core + l, "energy": first_e + 1}

    def is_owner(l):
        return (core == 1) & (place == 2 + l)

    def hand(src, dst, l, send, recv):
        @pl.when(is_owner(l))
        def _():
            pltpu.make_async_copy(src, dst, recv).start()

        @pl.when(jnp.logical_not(is_owner(l)))
        def _():
            remote(src, dst, send, recv, owner(l)).start()

    def handed(src, dst, l, send, recv):
        @pl.when(jnp.logical_not(is_owner(l)))
        def _():
            remote(src, dst, send, recv, owner(l)).wait_send()

    def wf_args(l):
        return wfo_v.at[l], wf_v.at[place], l, wf_s.at[l], wf_r.at[place]

    def we_args(l):
        return weo_v.at[l], we_v.at[place], l, we_s.at[l], we_r.at[place]

    def it_args(l):
        return it_v.at[l], itr_v.at[place], l, wf_s.at[l], wf_r.at[place]

    def a_args(c, l):
        return ao_v.at[c, l], x_v.at[c, 1 + place], l, a_s.at[2 * c + l], a_r.at[PARTS * place + c]

    def turn(given):
        for t in range(blocks):
            lanes = slice(t * nb, (t + 1) * nb)
            real = given[t, :nb, :].T
            imag = -(given[t, nb:, :].T)
            for s in range(blocks):
                cmt_v[s, :nb, lanes] = real[s * nb:(s + 1) * nb]
                cmt_v[s, nb:, lanes] = imag[s * nb:(s + 1) * nb]

    @pl.when((pos > 0) & early)
    def _():
        turn(cm_v)
        product_into(cmt_v, it_v.at[lead], wfo_v.at[lead])

    @pl.when(late | (pos == 0))
    def _():
        for l in range(2):
            @pl.when(lead != l)
            def _():
                load_it(l)

    @pl.when(late)
    def _():
        cmr_v[place] = cm_v[...]

    load_src.start()
    load_prev.start()
    pl.semaphore_wait(barrier, sum(jnp.where(there, 1, 0) for there, _ in partners))

    @pl.when(shifts_out)
    def _():
        send_cm.start()

    @pl.when(late)
    def _():
        for step in range(1, SPAN):
            ring_cm(step).start()

    def start_halos():
        for c in range(PARTS):
            @pl.when(e < energies - 1)
            def _():
                halo_right(c).start()

            @pl.when(e > 0)
            def _():
                halo_left(c).start()

    @pl.when(base == 0)
    def _():
        start_halos()

    @pl.when((pos > 0) & early)
    def _():
        for l in range(2):
            @pl.when(lead == l)
            def _():
                hand(*wf_args(l))
                load_it(1 - l)

        product_into(cmt_v, it_v.at[1 - lead], wfo_v.at[1 - lead])
        for l in range(2):
            @pl.when(lead != l)
            def _():
                hand(*wf_args(l))

    @pl.when(late)
    def _():
        for l in range(2):
            @pl.when(jnp.logical_not(is_far(l)))
            def _():
                hand(*it_args(l))

        for l in range(2):
            @pl.when(is_far(l))
            def _():
                hand(*it_args(l))

        start_halos()
        for slot in range(SPAN):
            @pl.when(slot != place)
            def _():
                ringed_cm(slot).wait_recv()
                for step in range(1, SPAN):
                    share_cm(slot, step).start()
    @pl.when(base == SPAN)
    def _():
        start_halos()

    @pl.when(early)
    def _():
        send_cm.wait_recv()
        for step in range(1, SPAN):
            share_cm(SPAN, step).start()

    @pl.when(early & (place < SPAN - 1))
    def _():
        pool_cm(SPAN)
        mate_cm(SPAN).start()

    near = F32(0)
    far = F32(0)
    for mode in range(off_ref.shape[0]):
        near = near + jnp.where(off_ref[mode] == 1, str_ref[mode], F32(0))
        far = far + jnp.where(off_ref[mode] == 2, str_ref[mode], F32(0))
    load_src.wait()
    load_prev.wait()

    @pl.when(e == 0)
    def _():
        hl_v[...] = jnp.zeros(hl_v.shape, BF16)

    @pl.when(e == energies - 1)
    def _():
        hr_v[...] = jnp.zeros(hr_v.shape, BF16)

    for c in range(PARTS):
        at = rows(c)

        @pl.when(e > 0)
        def _():
            halo_right(c).wait_recv()

        @pl.when(e < energies - 1)
        def _():
            halo_left(c).wait_recv()

        own = [prev_v[:, l, at, :].astype(F32) for l in range(2)]
        lo = [hl_v[:, l, at, :].astype(F32) for l in range(2)]
        hi = [hr_v[:, l, at, :].astype(F32) for l in range(2)]
        drives = (
            src_v[:, 0, at, :].astype(F32) + near * (own[1] + lo[1]) + far * (hi[0] + lo[0]),
            src_v[:, 1, at, :].astype(F32) + near * (hi[0] + own[0]) + far * (hi[1] + lo[1]),
        )
        for l in range(2):
            left = drives[l].astype(BF16).reshape(2 * width, no)
            real, imag = combined(jnp.dot(left, it_v[l], preferred_element_type=F32))
            ao_v[c, l, 0] = real.astype(BF16)
            ao_v[c, l, 1] = imag.astype(BF16)
            hand(*a_args(c, l))

    @pl.when(early & (place == SPAN - 1))
    def _():
        pool_cm(SPAN)
        mate_cm(SPAN).start()

    @pl.when(early)
    def _():
        mate_cm(SPAN).wait_recv()

        @pl.loop(0, 2)
        def _(n):
            l = jnp.where(n == 0, lead, 1 - lead)
            product_into(cmr_v.at[SPAN], it_v.at[l], weo_v.at[l])
            hand(*we_args(l))

    @pl.when(late)
    def _():
        for slot in range(SPAN):
            @pl.when(slot != place)
            def _():
                pool_cm(slot)
                mate_cm(slot).start()

        for slot in range(SPAN):
            @pl.when(slot != place)
            def _():
                mate_cm(slot).wait_recv()

    def by_arrival(n):
        return lax.rem(place + jnp.where(n < 2, n, 5 - n), SPAN)

    def pass_on(j):
        return remote(itr_v.at[j], itr_v.at[j], fw_s.at[j], fw_r.at[j], {"energy": first_e + 1 - core})

    def pass_back(j):
        return remote(we_v.at[j], we_v.at[j], fe_s.at[j], we_r.at[j], {"energy": first_e + 1 - core})

    @pl.when(late & (core == 1))
    def _():
        @pl.loop(0, SPAN)
        def _(turn_no):
            j = by_arrival(turn_no)
            remote(it_v.at[0], itr_v.at[j], wf_s.at[0], wf_r.at[j], owner(0)).wait_recv()

            @pl.when(j < SPAN - 1)
            def _():
                pass_on(j).start()

            turn(cmr_v.at[j])
            product_into(cmt_v, itr_v.at[j], wf_v.at[j])

        @pl.when(final_group)
        def _():
            for t in range(blocks):
                we_v[SPAN - 1, nb * t:nb * (t + 1), :no] = cmr_v[0, t, :nb]
                we_v[SPAN - 1, nb * t:nb * (t + 1), no:] = cmr_v[0, t, nb:]

        @pl.when(jnp.logical_not(final_group))
        def _():
            we_v[SPAN - 1] = itr_v[SPAN - 1]

    @pl.when(late & (core == 0))
    def _():
        @pl.loop(0, SPAN)
        def _(turn_no):
            j = by_arrival(turn_no)

            @pl.when(j < SPAN - 1)
            def _():
                pass_on(j).wait_recv()
                product_into(cmr_v.at[j + 1], itr_v.at[j], we_v.at[j])
                pass_back(j).start()

    def stepped(given, weights, added):
        left = given[...].reshape(2 * width, no)
        real, imag = combined(jnp.dot(left, weights[...], preferred_element_type=F32))
        return (real + added[0].astype(F32)).astype(BF16), (imag + added[1].astype(F32)).astype(BF16)

    def send_forward(c):
        return remote(x_v.at[c, SPAN], x_v.at[c, 0], f_s.at[c], f_r.at[c], {"cuts": pos + SPAN})

    def send_backward(c):
        return remote(u_v.at[c, 0], u_v.at[c, SPAN], b_s.at[c], b_r.at[c], {"cuts": pos - SPAN})

    def send_coupled(c):
        return remote(x_v.at[c, 0], u_v.at[c, SPAN], b_s.at[c], b_r.at[c], {"cuts": pos - SPAN})

    def out_at(c, l):
        return out_ref.at[:, l, 0, rows(c)]

    def is_home(j):
        return (place >= 2) & (j == place)

    def out_far(c, j, l):
        device = {"cuts": base + j, "energy": first_e + lax.div(place, 2)}
        return remote(u_v.at[c, j], out_at(c, l), o_s.at[SPAN * c + j], o_r.at[2 * c + l], device)

    def out_here(c, j, l):
        return pltpu.make_async_copy(u_v.at[c, j], out_at(c, l), o_r.at[2 * c + l])

    half_place = lax.rem(place, 2)

    @pl.when(core == 1)
    def _():
        for c in range(PARTS):
            for j in range(SPAN):
                remote(ao_v.at[c, 0], x_v.at[c, 1 + j], a_s.at[0], a_r.at[PARTS * j + c], owner(0)).wait_recv()

                @pl.when((j == 0) & (base > 0))
                def _():
                    send_forward(c).wait_recv()

                @pl.when(base + j > 0)
                def _(j=j):
                    if c == 0:
                        @pl.when(early)
                        def _():
                            remote(wfo_v.at[0], wf_v.at[j], wf_s.at[0], wf_r.at[j], owner(0)).wait_recv()

                    here = x_v.at[c, 1 + j]
                    here[0], here[1] = stepped(x_v.at[c, j], wf_v.at[j], here)

            @pl.when(base < cuts - SPAN)
            def _():
                send_forward(c).start()

        for c in range(PARTS):
            for back in range(SPAN):
                j = SPAN - 1 - back

                @pl.when((back == 0) & (base < cuts - SPAN))
                def _():
                    send_backward(c).wait_recv()

                @pl.when(base + j < last)
                def _():
                    if c == 0:
                        @pl.when(early | (back > 0))
                        def _():
                            remote(weo_v.at[0], we_v.at[j], we_s.at[0], we_r.at[j], owner(0)).wait_recv()

                    here = u_v.at[c, j]
                    here[0], here[1] = stepped(u_v.at[c, j + 1], we_v.at[j], x_v.at[c, 1 + j])

                @pl.when(base + j == last)
                def _():
                    u_v[c, j] = x_v[c, 1 + j]

                @pl.when((j == 0) & (base > 0) & jnp.logical_not(final_group))
                def _():
                    send_backward(c).start()

                @pl.when((j == 0) & final_group)
                def _():
                    left = u_v[c, 0].reshape(2 * width, no)
                    real, imag = combined(jnp.dot(left, we_v[SPAN - 1], preferred_element_type=F32))
                    x_v[c, 0, 0] = real.astype(BF16)
                    x_v[c, 0, 1] = imag.astype(BF16)
                    send_coupled(c).start()

                for l in range(2):
                    @pl.when((half_place == l) & is_home(j))
                    def _():
                        out_here(c, j, l).start()

                    @pl.when((half_place == l) & jnp.logical_not(is_home(j)))
                    def _():
                        out_far(c, j, l).start()

    for c in range(PARTS):
        for l in range(2):
            out_far(c, 0, l).wait_recv()
            handed(*a_args(c, l))

        @pl.when(core == 1)
        def _():
            @pl.loop(0, SPAN)
            def _(j):
                @pl.when(jnp.logical_not(is_home(j)))
                def _():
                    out_far(c, j, 0).wait_send()

            @pl.when(base < cuts - SPAN)
            def _():
                send_forward(c).wait_send()

            @pl.when(base > 0)
            def _():
                send_backward(c).wait_send()

        @pl.when(e < energies - 1)
        def _():
            halo_right(c).wait_send()

        @pl.when(e > 0)
        def _():
            halo_left(c).wait_send()

    @pl.when(shifts_out)
    def _():
        send_cm.wait_send()

    @pl.when(early)
    def _():
        for step in range(1, SPAN):
            share_cm(SPAN, step).wait_send()
        mate_cm(SPAN).wait_send()

    @pl.when((pos > 0) & early)
    def _():
        for l in range(2):
            handed(*wf_args(l))

    @pl.when(early)
    def _():
        for l in range(2):
            handed(*we_args(l))

    @pl.when(late)
    def _():
        for step in range(1, SPAN):
            ring_cm(step).wait_send()
        for l in range(2):
            handed(*it_args(l))
        for slot in range(SPAN):
            @pl.when(slot != place)
            def _():
                for step in range(1, SPAN):
                    share_cm(slot, step).wait_send()

                mate_cm(slot).wait_send()

        @pl.loop(0, SPAN - 1)
        def _(j):
            @pl.when(core == 1)
            def _():
                pass_on(j).wait_send()

            @pl.when(core == 0)
            def _():
                pass_back(j).wait_send()

def on_device(cuts, energies, inverse, coupling, pattern, source, previous, offsets, strength):
    no, nr = source.shape[4], source.shape[3]
    blocks = pattern.shape[-1]
    width = nr // PARTS
    dma = pltpu.SemaphoreType.DMA
    panel = pltpu.VMEM((2, 2, nr, no), BF16)
    stack = pltpu.VMEM((blocks, 2 * no // blocks, no), BF16)
    anywhere = pl.BlockSpec(memory_space=pl.ANY)
    scalars = pl.BlockSpec(memory_space=pltpu.SMEM)
    return pl.pallas_call(
        functools.partial(sweep_kernel, cuts, energies),
        name="sweeps",
        out_shape=jax.ShapeDtypeStruct(source.shape, BF16),
        in_specs=[anywhere, anywhere, scalars, anywhere, anywhere, scalars, scalars],
        out_specs=anywhere,
        scratch_shapes=[
            pltpu.VMEM((2, 2, no, no), BF16),
            pltpu.VMEM((2, no, 2 * no), BF16),
            pltpu.VMEM((2, no, no), BF16),
            stack, stack,
            pltpu.VMEM((SPAN + 1, blocks, 2 * no // blocks, no), BF16),
            pltpu.VMEM((2, no, 2 * no), BF16),
            pltpu.VMEM((2, no, 2 * no), BF16),
            pltpu.VMEM((SPAN, no, 2 * no), BF16),
            pltpu.VMEM((SPAN, no, 2 * no), BF16),
            pltpu.VMEM((SPAN, no, 2 * no), BF16),
            panel, panel, panel, panel,
            pltpu.VMEM((PARTS, 2, 2, width, no), BF16),
            pltpu.VMEM((PARTS, SPAN + 1, 2, width, no), BF16),
            pltpu.VMEM((PARTS, SPAN + 1, 2, width, no), BF16),
            dma((5,)),
            dma((PARTS,)), dma((PARTS,)), dma((PARTS,)), dma((PARTS,)),
            dma, dma,
            dma((SPAN - 1,)), dma((SPAN,)),
            dma(((SPAN - 1) * (SPAN + 1),)), dma(((SPAN - 1) * (SPAN + 1),)),
            dma((SPAN + 1,)), dma((SPAN + 1,)),
            dma((SPAN - 1,)), dma((SPAN - 1,)), dma((SPAN - 1,)),
            dma((2,)), dma((SPAN,)), dma((2,)), dma((SPAN,)),
            dma((2 * PARTS,)), dma((SPAN * PARTS,)),
            dma((PARTS,)), dma((PARTS,)), dma((PARTS,)), dma((PARTS,)),
            dma((SPAN * PARTS,)), dma((2 * PARTS,)),
        ],
        compiler_params=pltpu.CompilerParams(
            collective_id=0, has_side_effects=True, vmem_limit_bytes=60 << 20
        ),
    )(inverse, coupling, pattern, source, previous, offsets, strength)


def solution(mesh):
    return jax.shard_map(
        functools.partial(on_device, mesh.shape["cuts"], mesh.shape["energy"]),
        mesh=mesh,
        in_specs=(
            P(None, "energy", "cuts", None, None),
            P(None, "cuts", None, None),
            P("cuts", None, None),
            P(None, "energy", "cuts", None, None),
            P(None, "energy", "cuts", None, None),
            P(),
            P(),
        ),
        out_specs=P(None, "energy", "cuts", None, None),
        check_vma=False,
    )
```
